512 devices in a mesh: wide: 64 (over z, y), narrow: 8 (over x, core).
Axes of the slice: x: 4, y: 4, z: 16, core: 2. Of those that a mesh axis runs over, the one named last changes fastest.
Arguments:
- column_state: float32 [16, 4, 720896], P(None, None, ('wide', 'narrow')), may hold values from -6 to 6
- diffusivity: float32 [15, 720896], P(None, ('wide', 'narrow')), may hold values from 0.05 to 5
- row_len: int32 [128], replicated, may hold values from 2576 to 5136, as said below
- lat_rows: int32 [128], P('wide'), may hold values from 0 to 127, as said below
- wave_order: int32 [1280], replicated, may hold values from 0 to 1279, each once
- tile_map: int32 [512, 1408], P(('wide', 'narrow')), may hold values from 0 to 1407, each once within a row
Outputs:
- spectra: float32 [2, 64, 128, 1280], P(None, None, 'wide', 'narrow')
The draws below stay inside these ranges and needn't reach their ends.
Inputs may be any that keep to these rules, and one draw needn't show every extreme that they name: `row_len`: each length is 5136 minus a multiple of 4. `lat_rows`: a permutation of the row numbers. `wave_order`: a permutation of the wavenumbers. `tile_map`: each row is a permutation of the column slots.
All inputs are finite; a program needn't handle non-finite values.
Results may differ from the reference program's by a relative error of at most 0.0037.
Values may be sent and summed in bfloat16 or wider, within the bound.
No kernel may reach another device: no remote copies, remote signals or barrier semaphores. Data moves between devices by JAX's collectives and lax.ppermute only.
A program may use at most 64 MiB of HBM per device.

```python
import math
import jax
import jax.numpy as jnp
from jax import lax

F = 4
LMAX = 5136
LPAD = 5632
MW = 1280
LEV = 16
FL = 64
NROW = 128
PIECE = 22
COLS_DEV = 1408
NCOL = 720896
N_WIDE = 64
N_NARROW = 8


def length_steps(key):
    steps_drawn = jax.random.randint(key, (NROW,), 0, MW // 2 + 1, dtype=jnp.int32)
    steps_drawn = steps_drawn.at[0].set(0)
    steps_drawn = steps_drawn.at[1].set(MW // 2)
    return steps_drawn


def draw_row_len(key, part):
    steps_drawn = length_steps(key)
    return (LMAX - 4 * steps_drawn).astype(jnp.int32)


def draw_lat_rows(key, part):
    steps_drawn = length_steps(key)
    key = jax.random.fold_in(key, 7)
    jitter = jax.random.randint(key, (NROW,), 0, 8, dtype=jnp.int32)
    scores = (steps_drawn * 8 + jitter) * NROW + jnp.arange(NROW, dtype=jnp.int32)
    return jnp.argsort(scores, stable=True).astype(jnp.int32)


def block_scale(rng, dims, pieces, low, top_value):
    level = 1.0
    for position, shards_of in pieces:
        draws = jax.random.uniform(jax.random.fold_in(jax.random.fold_in(rng, 6), position), (shards_of,), jnp.float32, low / len(pieces), top_value / len(pieces))
        level = level * jnp.repeat(jnp.exp(draws), dims[position] // shards_of).reshape((-1,) + (1,) * (len(dims) - 1 - position))
    return level


def noise(stream_key, extent, deviation, bound, shards=(), held_as=jnp.bfloat16):
    result = deviation * jax.random.normal(stream_key, extent, jnp.float32)
    if shards:
        result = result * block_scale(stream_key, extent, shards, -0.22, 0.18)
    return jnp.clip(result, -bound, bound).astype(held_as)


def setup_inputs(seed: int = 0) -> dict:
    arg_keys = jax.random.split(jax.random.key(seed), 7)
    return {
        "column_state": noise(arg_keys[0], (LEV, F, NCOL), 1.0, 6.0, ((2, 512),), jnp.float32),
        "diffusivity": jnp.clip(jnp.exp(math.log(5.0) - 4.6051702 * jax.random.uniform(arg_keys[1], (LEV - 1, NCOL), jnp.float32) ** block_scale(arg_keys[1], (LEV - 1, NCOL), ((1, 512),), -0.2, 0.2)), 0.05, 5.0),
        "row_len": draw_row_len(jax.random.fold_in(arg_keys[6], 71), 0),
        "lat_rows": draw_lat_rows(jax.random.fold_in(arg_keys[6], 71), 0),
        "wave_order": jax.random.permutation(arg_keys[4], MW).astype(jnp.int32),
        "tile_map": jax.vmap(lambda own: jax.random.permutation(own, COLS_DEV))(jax.random.split(arg_keys[5], (N_WIDE * N_NARROW))).reshape((N_WIDE * N_NARROW, COLS_DEV)).astype(jnp.int32),
    }


def vertical_solve(column_state, diffusivity):
    zero_row = jnp.zeros_like(diffusivity[:1])
    below_coef = jnp.concatenate([zero_row, diffusivity], axis=0)
    above_coef = jnp.concatenate([diffusivity, zero_row], axis=0)

    def forward(carry_pair, level_items):
        ratio_prev, value_prev = carry_pair
        below, above, source = level_items
        pivot_value = 1.0 + below + above + below * ratio_prev
        ratio_now = -above / pivot_value
        value_now = (source + below * value_prev) / pivot_value
        return ((ratio_now, value_now), (ratio_now, value_now))
    start_pair = (jnp.zeros_like(diffusivity[0]), jnp.zeros_like(column_state[0]))
    unused, (ratios, values) = lax.scan(forward, start_pair, (below_coef, above_coef, column_state))

    def backward(next_value, level_items):
        ratio_now, value_now = level_items
        solved_level = value_now - ratio_now * next_value
        return (solved_level, solved_level)
    unused, solved = lax.scan(backward, jnp.zeros_like(column_state[0]), (ratios, values), reverse=True)
    return solved

def row_transform(row_values, length, wave_ids):
    slab_width = 512
    block_count = (length + slab_width - 1) // slab_width
    mode_count = wave_ids.shape[0]
    scale_angle = 2.0 * math.pi / length.astype(jnp.float32)
    positions = jnp.arange(slab_width, dtype=jnp.int32)
    residue = positions[:, None] * wave_ids[None, :] % length
    phase_angle = residue.astype(jnp.float32) * scale_angle
    base_table = jnp.concatenate([jnp.cos(phase_angle), -jnp.sin(phase_angle)], axis=1).astype(jnp.bfloat16)

    def add_block(block_index, sums_pair):
        real_sum, imag_sum = sums_pair
        first_slot = (block_index * slab_width).astype(jnp.int32)
        slab_values = lax.dynamic_slice_in_dim(row_values, first_slot, slab_width, 1)
        inside = first_slot + positions < length
        slab_values = jnp.where(inside[None, :], slab_values, jnp.zeros_like(slab_values))
        product = jnp.dot(slab_values, base_table, preferred_element_type=jnp.float32)
        cos_part = product[:, :mode_count]
        sin_part = product[:, mode_count:]
        shift_angle = (first_slot * wave_ids % length).astype(jnp.float32) * scale_angle
        twiddle_cos = jnp.cos(shift_angle)[None, :]
        twiddle_sin = jnp.sin(shift_angle)[None, :]
        real_sum = real_sum + twiddle_cos * cos_part + twiddle_sin * sin_part
        imag_sum = imag_sum + twiddle_cos * sin_part - twiddle_sin * cos_part
        return (real_sum, imag_sum)
    empty = jnp.zeros((row_values.shape[0], mode_count), jnp.float32)
    real_sum, imag_sum = lax.fori_loop(0, block_count, add_block, (empty, empty))
    return jnp.concatenate([real_sum, imag_sum], axis=1) * lax.rsqrt(length.astype(jnp.float32))

def reference(column_state, diffusivity, row_len, lat_rows, wave_order, tile_map):
    solved = vertical_solve(column_state, diffusivity)
    grid_cols = solved.astype(jnp.bfloat16).reshape(FL, N_WIDE * N_NARROW, COLS_DEV)
    grid_cols = jnp.take_along_axis(grid_cols, tile_map[None, :, :], axis=2)
    grid_cols = grid_cols.reshape(FL, N_WIDE, N_NARROW, N_WIDE, PIECE)
    row_slots = jnp.transpose(grid_cols, (3, 1, 2, 4, 0)).reshape(NROW, LPAD, FL)
    row_slots = jnp.transpose(row_slots, (0, 2, 1))
    lengths = row_len[lat_rows].astype(jnp.int32)

    def one_row(items):
        return row_transform(items[0], items[1], wave_order)
    spectra = lax.map(one_row, (row_slots, lengths))
    spectra = spectra.reshape(NROW, FL, 2, MW)
    return jnp.transpose(spectra, (2, 1, 0, 3))
```

```python
import math

import jax
import jax.numpy as jnp
from jax import lax
from jax.experimental import pallas as pl
from jax.experimental.pallas import tpu as pltpu
from jax.sharding import Mesh, PartitionSpec as P

LEV = 16
NF = 4
FL = 64
SETS = 64
PIECE = 22
TILE_COLS = 1408
CHUNK = 12
ROWS = SETS * CHUNK
HALF = ROWS // 2
OWN = 160
LANES = 384
VMEM = 40 * 1024 * 1024


def solve_kernel(state_ref, diff_ref, map_ref, out_ref, ratio_ref, value_ref, cols_ref, slots_ref, rows_ref):
    ratio = jnp.zeros((1, TILE_COLS), jnp.float32)
    value = jnp.zeros((NF, TILE_COLS), jnp.float32)
    below = jnp.zeros((1, TILE_COLS), jnp.float32)
    for lev in range(LEV):
        if lev < LEV - 1:
            above = diff_ref[lev : lev + 1, :]
        else:
            above = jnp.zeros((1, TILE_COLS), jnp.float32)
        inverse = 1.0 / (1.0 + below + above + below * ratio)
        ratio = -above * inverse
        value = (state_ref[lev] + below * value) * inverse
        ratio_ref[lev : lev + 1, :] = ratio
        value_ref[lev] = value
        below = above
    solved = value
    cols_ref[(LEV - 1) * NF : LEV * NF, :] = solved
    for lev in range(LEV - 2, -1, -1):
        solved = value_ref[lev] - ratio_ref[lev : lev + 1, :] * solved
        cols_ref[lev * NF : (lev + 1) * NF, :] = solved
    cols = cols_ref[...].astype(jnp.bfloat16)
    cols = jnp.concatenate([cols, cols], axis=0)
    step = 256
    for first in range(0, TILE_COLS, step):
        width = min(step, TILE_COLS - first)
        ids = lax.broadcasted_iota(jnp.int32, (TILE_COLS, width), 0)
        pick = jnp.where(ids == map_ref[0:1, first : first + width], 1.0, 0.0).astype(jnp.bfloat16)
        moved = jnp.dot(cols, pick, preferred_element_type=jnp.float32)
        slots_ref[first : first + width, :] = moved.T
    low_lane = lax.broadcasted_iota(jnp.int32, (PIECE // 2, 2 * FL), 1) < FL
    zero_row = jnp.zeros((1, 2 * FL), jnp.float32)
    for s in range(SETS):
        even = slots_ref[pl.ds(s * PIECE, PIECE // 2, stride=2), :]
        odd = slots_ref[pl.ds(s * PIECE + 1, PIECE // 2, stride=2), :]
        rows_ref[s * CHUNK : s * CHUNK + PIECE // 2, :] = jnp.where(low_lane, even, odd)
        rows_ref[s * CHUNK + PIECE // 2 : (s + 1) * CHUNK, :] = zero_row
    out_ref[...] = rows_ref[...].astype(jnp.bfloat16)


def cos_sin_turns(turns):
    square = turns * turns
    s = jnp.full_like(turns, -(math.pi**11) / math.factorial(11))
    for k, sign in ((9, 1.0), (7, -1.0), (5, 1.0), (3, -1.0), (1, 1.0)):
        s = s * square + sign * math.pi**k / math.factorial(k)
    s = s * turns
    c = jnp.full_like(turns, (math.pi**12) / math.factorial(12))
    for k, sign in ((10, -1.0), (8, 1.0), (6, -1.0), (4, 1.0), (2, -1.0), (0, 1.0)):
        c = c * square + sign * math.pi**k / math.factorial(k)
    return 1.0 - 2.0 * s * s, 2.0 * s * c


def turns_of(product, length, inverse):
    return (product - jnp.floor(product * inverse + 0.5) * length) * inverse


def row_lengths(len_ref, lat_ref, r):
    return len_ref[lat_ref[r]]


def table_kernel(len_ref, lat_ref, pos_ref, wave_ref, table_ref, twiddle_ref):
    pos = pos_ref[0]
    core = lax.rem(pos, 2)
    other = pos + 1 - 2 * core
    own = wave_ref[pl.ds(pos, 1), :]
    theirs = wave_ref[pl.ds(other, 1), :]
    waves = jnp.concatenate([own, theirs, jnp.zeros((1, LANES - 2 * OWN), jnp.int32)], axis=1)
    waves = waves.astype(jnp.float32)
    block = 16
    for r in range(2):
        length = jnp.full((1, LANES), row_lengths(len_ref, lat_ref, r), jnp.int32).astype(jnp.float32)
        inverse = 1.0 / length
        scale = lax.rsqrt(length)
        scale = scale * (1.5 - 0.5 * length * scale * scale)
        for first in range(0, HALF, block):
            row = (lax.broadcasted_iota(jnp.int32, (block, LANES), 0) + first).astype(jnp.float32)
            group = jnp.floor((row + 0.5) * (1.0 / CHUNK))
            slot = 8.0 * PIECE * group + 2.0 * (row - CHUNK * group)
            cosine, sine = cos_sin_turns(turns_of(slot * waves, length, inverse))
            table_ref[r, first : first + block, 0:LANES] = cosine.astype(jnp.bfloat16)
            table_ref[r, first : first + block, LANES:] = (-sine).astype(jnp.bfloat16)
        item = lax.broadcasted_iota(jnp.int32, (8, LANES), 0)
        shift = 2 * PIECE * (item // 2) + item % 2 + PIECE * core
        cosine, sine = cos_sin_turns(turns_of(shift.astype(jnp.float32) * waves, length, inverse))
        twiddle_ref[2 * r] = cosine * scale
        twiddle_ref[2 * r + 1] = sine * scale


def transform_kernel(len_ref, lat_ref, pos_ref, rows_ref, table_ref, twiddle_ref, own_ref, theirs_ref):
    core = lax.rem(pos_ref[0], 2)
    row = lax.broadcasted_iota(jnp.int32, (HALF, 2 * FL), 0)
    lane = lax.broadcasted_iota(jnp.int32, (HALF, 2 * FL), 1)
    group = row // CHUNK
    inner = row - CHUNK * group
    slot = 8 * PIECE * group + 2 * inner + jnp.where(lane >= FL, 1, 0)
    slot = jnp.where(inner == CHUNK - 1, 1 << 20, slot)
    for r in range(2):
        length = row_lengths(len_ref, lat_ref, r)
        real = jnp.zeros((FL, LANES), jnp.float32)
        imag = jnp.zeros((FL, LANES), jnp.float32)
        for x in range(4):
            inside = slot < length - 2 * PIECE * x - PIECE * core
            values = rows_ref[x, r * HALF : (r + 1) * HALF, :].astype(jnp.float32)
            values = jnp.where(inside, values, 0.0).T.astype(jnp.bfloat16)
            product = jnp.dot(values, table_ref[r], preferred_element_type=jnp.float32)
            for p in range(2):
                cos_part = product[p * FL : (p + 1) * FL, 0:LANES]
                sin_part = product[p * FL : (p + 1) * FL, LANES:]
                tc = twiddle_ref[2 * r, 2 * x + p : 2 * x + p + 1, :]
                ts = twiddle_ref[2 * r + 1, 2 * x + p : 2 * x + p + 1, :]
                real = real + tc * cos_part + ts * sin_part
                imag = imag + tc * sin_part - ts * cos_part
        own_ref[0, r] = real[:, 0:OWN]
        own_ref[1, r] = imag[:, 0:OWN]
        theirs_ref[0, r] = real[:, OWN : 2 * OWN]
        theirs_ref[1, r] = imag[:, OWN : 2 * OWN]


def add_kernel(own_ref, got_ref, out_ref):
    for part in range(2):
        for r in range(2):
            out_ref[part, :, r, :] = own_ref[part, r] + got_ref[part, r]


def body(column_state, diffusivity, row_len, lat_rows, wave_order, tile_map):
    f32, bf16 = jnp.float32, jnp.bfloat16
    pos = (2 * lax.axis_index("x") + lax.axis_index("core")).astype(jnp.int32).reshape(1)
    smem = pl.BlockSpec(memory_space=pltpu.SMEM)
    vmem = pl.BlockSpec(memory_space=pltpu.VMEM)
    params = pltpu.CompilerParams(vmem_limit_bytes=VMEM)
    rows = pl.pallas_call(
        solve_kernel,
        out_shape=jax.ShapeDtypeStruct((ROWS, 2 * FL), bf16),
        in_specs=[vmem] * 3,
        out_specs=vmem,
        scratch_shapes=[
            pltpu.VMEM((LEV, TILE_COLS), f32),
            pltpu.VMEM((LEV, NF, TILE_COLS), f32),
            pltpu.VMEM((FL, TILE_COLS), f32),
            pltpu.VMEM((TILE_COLS, 2 * FL), f32),
            pltpu.VMEM((ROWS, 2 * FL), f32),
        ],
        compiler_params=params,
        name="solve",
    )(column_state, diffusivity, tile_map)
    table, twiddle = pl.pallas_call(
        table_kernel,
        out_shape=[
            jax.ShapeDtypeStruct((2, HALF, 2 * LANES), bf16),
            jax.ShapeDtypeStruct((4, 8, LANES), f32),
        ],
        in_specs=[smem, smem, smem, vmem],
        out_specs=[vmem, vmem],
        compiler_params=params,
        cost_estimate=pl.CostEstimate(flops=20_000_000, bytes_accessed=1_300_000, transcendentals=0),
        name="tables",
    )(row_len, lat_rows, pos, wave_order.reshape(8, OWN))
    rows = rows.reshape(SETS, CHUNK // 2, 2, 2 * FL)
    rows = lax.all_to_all(rows, ("z", "y"), split_axis=0, concat_axis=0, tiled=True)
    rows = rows.reshape(ROWS, 2 * FL)
    rows = lax.all_gather(rows, "x", axis=0, tiled=False)
    half = jax.ShapeDtypeStruct((2, 2, FL, OWN), f32)
    own, theirs = pl.pallas_call(
        transform_kernel,
        out_shape=[half, half],
        in_specs=[smem, smem, smem, vmem, vmem, vmem],
        out_specs=[vmem, vmem],
        compiler_params=params,
        name="transform",
    )(row_len, lat_rows, pos, rows, table, twiddle)
    got = lax.ppermute(theirs, "core", [(0, 1), (1, 0)])
    return pl.pallas_call(
        add_kernel,
        out_shape=jax.ShapeDtypeStruct((2, FL, 2, OWN), f32),
        in_specs=[vmem, vmem],
        out_specs=vmem,
        compiler_params=params,
        name="add",
    )(own, got)


def solution(mesh):
    chips = Mesh(mesh.devices.reshape(16, 4, 4, 2), ("z", "y", "x", "core"))
    columns = ("z", "y", "x", "core")
    return jax.shard_map(
        body,
        mesh=chips,
        in_specs=(
            P(None, None, columns),
            P(None, columns),
            P(),
            P(("z", "y")),
            P(),
            P(columns, None),
        ),
        out_specs=P(None, None, ("z", "y"), ("x", "core")),
        check_vma=False,
    )
```

```python
import math

import jax
import jax.numpy as jnp
from jax import lax
from jax.experimental import pallas as pl
from jax.experimental.pallas import tpu as pltpu
from jax.sharding import Mesh, PartitionSpec as P

LEV = 16
NF = 4
FL = 64
SETS = 64
PIECE = 22
TILE_COLS = 1408
CHUNK = 12
ROWS = SETS * CHUNK
HALF = ROWS // 2
BASE = HALF // 2
OWN = 160
MAIN = 128
TAIL = OWN - MAIN
PEERS = 8
CHIPS = 4
MODES = PEERS * OWN
SHARE = CHIPS * OWN
VMEM = 40 * 1024 * 1024
SOLVE_VMEM = 62 * 1024 * 1024


def solve_kernel(state_hbm, diff_hbm, map_hbm, out_ref, state_ref, diff_ref, map_ref, ratio_ref, value_ref, cols_ref, pick_ref, slots_ref, rows_ref, sems):
    copies = [pltpu.make_async_copy(map_hbm, map_ref, sems.at[0]), pltpu.make_async_copy(diff_hbm, diff_ref, sems.at[1])]
    for part in range(4):
        levels = pl.ds(4 * part, 4)
        copies.append(pltpu.make_async_copy(state_hbm.at[levels], state_ref.at[levels], sems.at[2 + part]))
    for copy in copies:
        copy.start()
    copies[0].wait()
    for first in range(0, TILE_COLS, 128):
        ids = lax.broadcasted_iota(jnp.int32, (TILE_COLS, 128), 0)
        pick = jnp.where(ids == map_ref[0:1, first : first + 128], 1.0, 0.0)
        pick_ref[:, first : first + 128] = pick.astype(jnp.bfloat16)
    copies[1].wait()
    ratio = jnp.zeros((1, TILE_COLS), jnp.float32)
    value = jnp.zeros((NF, TILE_COLS), jnp.float32)
    below = jnp.zeros((1, TILE_COLS), jnp.float32)
    for lev in range(LEV):
        if lev % 4 == 0:
            copies[2 + lev // 4].wait()
        if lev < LEV - 1:
            above = diff_ref[lev : lev + 1, :]
        else:
            above = jnp.zeros((1, TILE_COLS), jnp.float32)
        inverse = 1.0 / (1.0 + below + above + below * ratio)
        ratio = -above * inverse
        value = (state_ref[lev] + below * value) * inverse
        ratio_ref[lev : lev + 1, :] = ratio
        value_ref[lev] = value
        below = above
    solved = value
    cols_ref[(LEV - 1) * NF : LEV * NF, :] = solved
    for lev in range(LEV - 2, -1, -1):
        solved = value_ref[lev] - ratio_ref[lev : lev + 1, :] * solved
        cols_ref[lev * NF : (lev + 1) * NF, :] = solved
    cols = cols_ref[...].astype(jnp.bfloat16)
    cols = jnp.concatenate([cols, cols], axis=0)
    step = 256
    for first in range(0, TILE_COLS, step):
        width = min(step, TILE_COLS - first)
        moved = jnp.dot(cols, pick_ref[:, first : first + width], preferred_element_type=jnp.float32)
        slots_ref[first : first + width, :] = moved.T
    low_lane = lax.broadcasted_iota(jnp.int32, (PIECE // 2, 2 * FL), 1) < FL
    zero_row = jnp.zeros((1, 2 * FL), jnp.float32)
    for s in range(SETS):
        even = slots_ref[pl.ds(s * PIECE, PIECE // 2, stride=2), :]
        odd = slots_ref[pl.ds(s * PIECE + 1, PIECE // 2, stride=2), :]
        both = jnp.where(low_lane, even, odd)
        rows_ref[s * CHUNK : s * CHUNK + PIECE // 2, :] = both
        rows_ref[s * CHUNK + PIECE // 2 : (s + 1) * CHUNK, :] = zero_row
    out_ref[...] = rows_ref[...].astype(jnp.bfloat16)


def cos_sin_turns(turns):
    square = turns * turns
    s = jnp.full_like(turns, -(math.pi**11) / math.factorial(11))
    for k, sign in ((9, 1.0), (7, -1.0), (5, 1.0), (3, -1.0), (1, 1.0)):
        s = s * square + sign * math.pi**k / math.factorial(k)
    s = s * turns
    c = jnp.full_like(turns, (math.pi**12) / math.factorial(12))
    for k, sign in ((10, -1.0), (8, 1.0), (6, -1.0), (4, 1.0), (2, -1.0), (0, 1.0)):
        c = c * square + sign * math.pi**k / math.factorial(k)
    return 1.0 - 2.0 * s * s, 2.0 * s * c


def turns_of(product, length, inverse):
    return (product - jnp.floor(product * inverse + 0.5) * length) * inverse


def row_lengths(len_ref, lat_ref, r):
    return len_ref[lat_ref[r]]


def table_kernel(len_ref, lat_ref, pos_ref, wave_ref, table_ref, twiddle_ref, limit_ref):
    core = lax.rem(pos_ref[0], 2)
    waves = []
    for side in (core, 1 - core):
        rows_of = [wave_ref[pl.ds(2 * chip + side, 1), :] for chip in range(CHIPS)]
        waves += [row[:, 0:MAIN] for row in rows_of] + [row[:, MAIN:OWN] for row in rows_of]
    waves = jnp.concatenate(waves, axis=1).astype(jnp.float32)
    rows = 8
    for r in range(2):
        limit_ref[r] = jnp.full((8, 2 * FL), row_lengths(len_ref, lat_ref, r) - PIECE * pos_ref[0], jnp.int32)
        length = jnp.full((1, MODES), row_lengths(len_ref, lat_ref, r), jnp.int32).astype(jnp.float32)
        inverse = 1.0 / length
        scale = lax.rsqrt(length)
        scale = scale * (1.5 - 0.5 * length * scale * scale)

        def some_rows(step, carry):
            first = pl.multiple_of(step * 2 * rows, 2 * rows)
            cosines, sines = [], []
            for part in range(2):
                row = lax.broadcasted_iota(jnp.int32, (rows, MODES), 0) + (first + part * rows)
                row = row.astype(jnp.float32)
                group = jnp.floor((row + 0.5) * (1.0 / CHUNK))
                slot = 8.0 * PIECE * group + 2.0 * (row - CHUNK * group)
                cosine, sine = cos_sin_turns(turns_of(slot * waves, length, inverse))
                cosines.append(cosine)
                sines.append(-sine)
            table_ref[r, pl.ds(first, 2 * rows), 0:MODES] = jnp.concatenate(cosines, axis=0).astype(jnp.bfloat16)
            table_ref[r, pl.ds(first, 2 * rows), MODES:] = jnp.concatenate(sines, axis=0).astype(jnp.bfloat16)
            return carry

        lax.fori_loop(0, BASE // (2 * rows), some_rows, 0)
        item = lax.broadcasted_iota(jnp.int32, (8, MODES), 0)
        shift = (BASE // CHUNK) * 8 * PIECE * (item // 2) + item % 2 + PIECE * pos_ref[0]
        cosine, sine = cos_sin_turns(turns_of(shift.astype(jnp.float32) * waves, length, inverse))
        twiddle_ref[2 * r] = cosine * scale
        twiddle_ref[2 * r + 1] = sine * scale


def combine(values, table_ref, twiddle_ref, r, first, width):
    lanes = slice(first, first + width)
    cos_all = jnp.dot(values, table_ref[r, :, lanes], preferred_element_type=jnp.float32)
    sin_lanes = slice(MODES + first, MODES + first + width)
    sin_all = jnp.dot(values, table_ref[r, :, sin_lanes], preferred_element_type=jnp.float32)
    real = jnp.zeros((FL, width), jnp.float32)
    imag = jnp.zeros((FL, width), jnp.float32)
    for item in range(4):
        cos_part = cos_all[item * FL : (item + 1) * FL]
        sin_part = sin_all[item * FL : (item + 1) * FL]
        tc = twiddle_ref[2 * r, item : item + 1, lanes]
        ts = twiddle_ref[2 * r + 1, item : item + 1, lanes]
        real = real + tc * cos_part + ts * sin_part
        imag = imag + tc * sin_part - ts * cos_part
    return real, imag


def share_of(values_of, start, table_ref, twiddle_ref, out_ref, tails_ref):
    for r in range(2):
        values = values_of(r)
        for pair in range(CHIPS // 2):
            sums = combine(values, table_ref, twiddle_ref, r, start + 2 * MAIN * pair, 2 * MAIN)
            for part in range(2):
                k = 2 * part + r
                for half in range(2):
                    block = sums[part][:, half * MAIN : (half + 1) * MAIN]
                    out_ref[2 * pair + half, k * FL : (k + 1) * FL, :] = block.astype(out_ref.dtype)
        sums = combine(values, table_ref, twiddle_ref, r, start + CHIPS * MAIN, CHIPS * TAIL)
        for part in range(2):
            tails_ref[2 * part + r] = sums[part]
    for chip in range(CHIPS):
        tail = [tails_ref[k, :, TAIL * chip : TAIL * (chip + 1)] for k in range(4)]
        out_ref[chip, 4 * FL :, :] = jnp.concatenate(tail, axis=1).astype(out_ref.dtype)


def other_kernel(rows_ref, limit_ref, table_ref, twiddle_ref, out_ref, values_ref, tails_ref):
    row = lax.broadcasted_iota(jnp.int32, (HALF, 2 * FL), 0)
    lane = lax.broadcasted_iota(jnp.int32, (HALF, 2 * FL), 1)
    group = row // CHUNK
    inner = row - CHUNK * group
    slot = 8 * PIECE * group + 2 * inner + jnp.where(lane >= FL, 1, 0)
    slot = jnp.where(inner == CHUNK - 1, 1 << 20, slot)

    def values_of(r):
        inside = slot < limit_ref[r, 0:1, :]
        values = jnp.where(inside, rows_ref[r * HALF : (r + 1) * HALF, :].astype(jnp.float32), 0.0)
        values = jnp.concatenate([values[:BASE].T, values[BASE:].T], axis=0).astype(jnp.bfloat16)
        values_ref[r] = values
        return values

    share_of(values_of, SHARE, table_ref, twiddle_ref, out_ref, tails_ref)


def own_kernel(values_ref, table_ref, twiddle_ref, out_ref, tails_ref):
    share_of(lambda r: values_ref[r], 0, table_ref, twiddle_ref, out_ref, tails_ref)


def pair_kernel(own_ref, got_ref, out_ref):
    for chip in range(CHIPS):
        out_ref[chip] = (own_ref[chip] + got_ref[chip].astype(jnp.float32)).astype(jnp.bfloat16)


def add_kernel(got_ref, out_ref):
    def total(start, stop):
        sums = got_ref[0, start:stop, :].astype(jnp.float32)
        for chip in range(1, CHIPS):
            sums = sums + got_ref[chip, start:stop, :].astype(jnp.float32)
        return sums

    tail = total(4 * FL, 5 * FL)
    for part in range(2):
        for r in range(2):
            k = 2 * part + r
            main = total(k * FL, (k + 1) * FL)
            both = jnp.concatenate([main, tail[:, k * TAIL : (k + 1) * TAIL]], axis=1)
            out_ref[part, :, r, :] = both


def body(column_state, diffusivity, row_len, lat_rows, wave_order, tile_map):
    f32, bf16 = jnp.float32, jnp.bfloat16
    pos = (2 * lax.axis_index("x") + lax.axis_index("core")).astype(jnp.int32).reshape(1)
    smem = pl.BlockSpec(memory_space=pltpu.SMEM)
    vmem = pl.BlockSpec(memory_space=pltpu.VMEM)
    hbm = pl.BlockSpec(memory_space=pltpu.HBM)
    params = pltpu.CompilerParams(vmem_limit_bytes=VMEM)
    rows = pl.pallas_call(
        solve_kernel,
        out_shape=jax.ShapeDtypeStruct((ROWS, 2 * FL), bf16),
        in_specs=[hbm] * 3,
        out_specs=vmem,
        scratch_shapes=[
            pltpu.VMEM((LEV, NF, TILE_COLS), f32),
            pltpu.VMEM((LEV - 1, TILE_COLS), f32),
            pltpu.VMEM((1, TILE_COLS), jnp.int32),
            pltpu.VMEM((LEV, TILE_COLS), f32),
            pltpu.VMEM((LEV, NF, TILE_COLS), f32),
            pltpu.VMEM((FL, TILE_COLS), f32),
            pltpu.VMEM((TILE_COLS, TILE_COLS), bf16),
            pltpu.VMEM((TILE_COLS, 2 * FL), f32),
            pltpu.VMEM((ROWS, 2 * FL), f32),
            pltpu.SemaphoreType.DMA((6,)),
        ],
        compiler_params=pltpu.CompilerParams(vmem_limit_bytes=SOLVE_VMEM),
        name="solve",
    )(column_state, diffusivity, tile_map)
    table, twiddle, limit = pl.pallas_call(
        table_kernel,
        out_shape=[
            jax.ShapeDtypeStruct((2, BASE, 2 * MODES), bf16),
            jax.ShapeDtypeStruct((4, 8, MODES), f32),
            jax.ShapeDtypeStruct((2, 8, 2 * FL), jnp.int32),
        ],
        in_specs=[smem, smem, smem, vmem],
        out_specs=[vmem, vmem, vmem],
        compiler_params=params,
        cost_estimate=pl.CostEstimate(flops=40_000_000, bytes_accessed=2_200_000, transcendentals=0),
        name="tables",
    )(row_len, lat_rows, pos, wave_order.reshape(PEERS, OWN))
    rows = rows.reshape(SETS, CHUNK // 2, 2, 2 * FL)
    rows = lax.all_to_all(rows, ("z", "y"), split_axis=0, concat_axis=0, tiled=True)
    rows = rows.reshape(ROWS, 2 * FL)
    rows, table, twiddle, limit = lax.optimization_barrier((rows, table, twiddle, limit))
    tails = pltpu.VMEM((4, FL, CHIPS * TAIL), f32)
    other, values = pl.pallas_call(
        other_kernel,
        out_shape=[
            jax.ShapeDtypeStruct((CHIPS, 5 * FL, MAIN), bf16),
            jax.ShapeDtypeStruct((2, 4 * FL, BASE), bf16),
        ],
        in_specs=[vmem] * 4,
        out_specs=[vmem] * 2,
        scratch_shapes=[tails],
        compiler_params=params,
        name="transform_other",
    )(rows, limit, table, twiddle)
    got = lax.ppermute(other, "core", [(0, 1), (1, 0)])
    own = pl.pallas_call(
        own_kernel,
        out_shape=jax.ShapeDtypeStruct((CHIPS, 5 * FL, MAIN), f32),
        in_specs=[vmem] * 3,
        out_specs=vmem,
        scratch_shapes=[tails],
        compiler_params=params,
        cost_estimate=pl.CostEstimate(flops=500_000_000, bytes_accessed=2_000_000, transcendentals=0),
        name="transform_own",
    )(values, table, twiddle)
    sums = pl.pallas_call(
        pair_kernel,
        out_shape=jax.ShapeDtypeStruct((CHIPS, 5 * FL, MAIN), bf16),
        in_specs=[vmem] * 2,
        out_specs=vmem,
        compiler_params=params,
        name="pair",
    )(own, got)
    sums = lax.all_to_all(sums, "x", split_axis=0, concat_axis=0, tiled=True)
    return pl.pallas_call(
        add_kernel,
        out_shape=jax.ShapeDtypeStruct((2, FL, 2, OWN), f32),
        in_specs=[vmem],
        out_specs=vmem,
        compiler_params=params,
        name="add",
    )(sums)


def solution(mesh):
    chips = Mesh(mesh.devices.reshape(16, 4, 4, 2), ("z", "y", "x", "core"))
    columns = ("z", "y", "x", "core")
    return jax.shard_map(
        body,
        mesh=chips,
        in_specs=(
            P(None, None, columns),
            P(None, columns),
            P(),
            P(("z", "y")),
            P(),
            P(columns, None),
        ),
        out_specs=P(None, None, ("z", "y"), ("x", "core")),
        check_vma=False,
    )
```

```python
import math

import jax
import jax.numpy as jnp
from jax import lax
from jax.experimental import pallas as pl
from jax.experimental.pallas import tpu as pltpu
from jax.sharding import Mesh, PartitionSpec as P

LEV = 16
NF = 4
FL = 64
SETS = 64
PIECE = 22
TILE_COLS = 1408
CHUNK = 12
ROWS = SETS * CHUNK
HALF = ROWS // 2
BASE = HALF // 2
OWN = 160
MAIN = 128
TAIL = OWN - MAIN
PEERS = 8
CHIPS = 4
ROW_TILES = 4
Z_ORDER = (0, 15, 1, 14, 2, 13, 3, 12, 4, 11, 5, 10, 6, 9, 7, 8)
ORDER = tuple(z * ROW_TILES + y for z in Z_ORDER for y in range(ROW_TILES))
SHARE = CHIPS * OWN
VMEM = 40 * 1024 * 1024
SOLVE_VMEM = 62 * 1024 * 1024


def lane_gather(values, lanes):
    return jnp.take_along_axis(values, lanes, axis=1, mode="promise_in_bounds")


def solve_kernel(state_hbm, diff_hbm, map_hbm, out_ref, state_ref, diff_ref, map_ref, ratio_ref, value_ref, cols_ref, pick_ref, rows_ref, sems):
    copies = [pltpu.make_async_copy(map_hbm, map_ref, sems.at[0]), pltpu.make_async_copy(diff_hbm, diff_ref, sems.at[1])]
    for part in range(4):
        levels = pl.ds(4 * part, 4)
        copies.append(pltpu.make_async_copy(state_hbm.at[levels], state_ref.at[levels], sems.at[2 + part]))
    for copy in copies:
        copy.start()
    copies[0].wait()
    tiles = ROWS // 128
    for part in range(2):
        for tile in range(tiles):
            place = (lax.broadcasted_iota(jnp.int32, (8, 128), 1) + 128 * tile).astype(jnp.float32)
            chunk = jnp.floor((place + 0.5) * (1.0 / CHUNK))
            inner = place - CHUNK * chunk
            slot = (PIECE * chunk + 2.0 * inner + part).astype(jnp.int32)
            lo_tile = (PIECE * (128 * tile // CHUNK)) // 128
            hi_tile = min(TILE_COLS // 128 - 1, (PIECE * ((128 * tile + 127) // CHUNK) + PIECE - 1) // 128)
            column = jnp.full((8, 128), -1, jnp.int32)
            for k in range(lo_tile, hi_tile + 1):
                entries = jnp.broadcast_to(map_ref[0:1, 128 * k : 128 * (k + 1)], (8, 128))
                found = lane_gather(entries, jnp.bitwise_and(slot, 127))
                column = jnp.where(slot // 128 == k, found, column)
            pick_ref[tiles * part + tile] = jnp.where(inner < PIECE // 2, column, -1)
    copies[1].wait()
    ratio = jnp.zeros((1, TILE_COLS), jnp.float32)
    value = jnp.zeros((NF, TILE_COLS), jnp.float32)
    below = jnp.zeros((1, TILE_COLS), jnp.float32)
    for lev in range(LEV):
        if lev % 4 == 0:
            copies[2 + lev // 4].wait()
        if lev < LEV - 1:
            above = diff_ref[lev : lev + 1, :]
        else:
            above = jnp.zeros((1, TILE_COLS), jnp.float32)
        inverse = 1.0 / (1.0 + below + above + below * ratio)
        ratio = -above * inverse
        value = (state_ref[lev] + below * value) * inverse
        ratio_ref[lev : lev + 1, :] = ratio
        value_ref[lev] = value
        below = above
    solved = value
    cols_ref[(LEV - 1) * NF : LEV * NF, :] = solved
    for lev in range(LEV - 2, -1, -1):
        solved = value_ref[lev] - ratio_ref[lev : lev + 1, :] * solved
        cols_ref[lev * NF : (lev + 1) * NF, :] = solved
    for tile in range(tiles):
        blocks = []
        for part in range(2):
            column = pick_ref[tiles * part + tile]
            lane = jnp.bitwise_and(column, 127)
            source = jnp.right_shift(column, 7)
            hits = [source == k for k in range(TILE_COLS // 128)]
            for first in range(0, FL, 8):
                block = jnp.zeros((8, 128), jnp.float32)
                for k in range(TILE_COLS // 128):
                    found = lane_gather(cols_ref[first : first + 8, 128 * k : 128 * (k + 1)], lane)
                    block = jnp.where(hits[k], found, block)
                blocks.append(block)
        rows_ref[128 * tile : 128 * (tile + 1), :] = jnp.concatenate(blocks, axis=0).T
    step = ROW_TILES * CHUNK
    for place, z in enumerate(Z_ORDER):
        block = rows_ref[step * z : step * (z + 1), :]
        out_ref[step * place : step * (place + 1), :] = block.astype(jnp.bfloat16)


def cos_sin_turns(turns):
    square = turns * turns
    s = jnp.full_like(turns, -(math.pi**11) / math.factorial(11))
    for k, sign in ((9, 1.0), (7, -1.0), (5, 1.0), (3, -1.0), (1, 1.0)):
        s = s * square + sign * math.pi**k / math.factorial(k)
    s = s * turns
    c = jnp.full_like(turns, (math.pi**12) / math.factorial(12))
    for k, sign in ((10, -1.0), (8, 1.0), (6, -1.0), (4, 1.0), (2, -1.0), (0, 1.0)):
        c = c * square + sign * math.pi**k / math.factorial(k)
    return 1.0 - 2.0 * s * s, 2.0 * s * c


def turns_of(product, length, inverse):
    return (product - jnp.floor(product * inverse + 0.5) * length) * inverse


def row_lengths(len_ref, lat_ref, r):
    return len_ref[lat_ref[r]]


def table_kernel(len_ref, lat_ref, pos_ref, wave_ref, table_ref, twiddle_ref, limit_ref):
    core = lax.rem(pos_ref[0], 2)
    rows_of = [wave_ref[pl.ds(2 * chip + core, 1), :] for chip in range(CHIPS)]
    waves = [row[:, 0:MAIN] for row in rows_of] + [row[:, MAIN:OWN] for row in rows_of]
    waves = jnp.concatenate(waves, axis=1).astype(jnp.float32)
    pieces = (pos_ref[0], pos_ref[0] + 1 - 2 * core)
    rows = 8
    for r in range(2):
        count = row_lengths(len_ref, lat_ref, r)
        for source in range(2):
            limit_ref[2 * source + r] = jnp.full((8, 2 * FL), count - PIECE * pieces[source], jnp.int32)
        length = jnp.full((1, SHARE), count, jnp.int32).astype(jnp.float32)
        inverse = 1.0 / length
        scale = lax.rsqrt(length)
        scale = scale * (1.5 - 0.5 * length * scale * scale)

        def some_rows(step, carry):
            first = pl.multiple_of(step * 2 * rows, 2 * rows)
            cosines, sines = [], []
            for part in range(2):
                row = lax.broadcasted_iota(jnp.int32, (rows, SHARE), 0) + (first + part * rows)
                row = row.astype(jnp.float32)
                group = jnp.floor((row + 0.5) * (1.0 / CHUNK))
                slot = 8.0 * PIECE * group + 2.0 * (row - CHUNK * group)
                cosine, sine = cos_sin_turns(turns_of(slot * waves, length, inverse))
                cosines.append(cosine)
                sines.append(-sine)
            table_ref[r, pl.ds(first, 2 * rows), 0:SHARE] = jnp.concatenate(cosines, axis=0).astype(jnp.bfloat16)
            table_ref[r, pl.ds(first, 2 * rows), SHARE:] = jnp.concatenate(sines, axis=0).astype(jnp.bfloat16)
            return carry

        lax.fori_loop(0, BASE // (2 * rows), some_rows, 0)
        item = lax.broadcasted_iota(jnp.int32, (8, SHARE), 0)
        shift = (BASE // CHUNK) * 8 * PIECE * (item // 2 % 2) + item % 2
        shift = shift + PIECE * jnp.where(item < 4, pieces[0], pieces[1])
        cosine, sine = cos_sin_turns(turns_of(shift.astype(jnp.float32) * waves, length, inverse))
        twiddle_ref[2 * r] = cosine * scale
        twiddle_ref[2 * r + 1] = sine * scale


def combine(values, table_ref, twiddle_ref, source, r, first, width):
    lanes = slice(first, first + width)
    cos_all = jnp.dot(values, table_ref[r, :, lanes], preferred_element_type=jnp.float32)
    sin_lanes = slice(SHARE + first, SHARE + first + width)
    sin_all = jnp.dot(values, table_ref[r, :, sin_lanes], preferred_element_type=jnp.float32)
    real = jnp.zeros((FL, width), jnp.float32)
    imag = jnp.zeros((FL, width), jnp.float32)
    for item in range(4):
        cos_part = cos_all[item * FL : (item + 1) * FL]
        sin_part = sin_all[item * FL : (item + 1) * FL]
        k = 4 * source + item
        tc = twiddle_ref[2 * r, k : k + 1, lanes]
        ts = twiddle_ref[2 * r + 1, k : k + 1, lanes]
        real = real + tc * cos_part + ts * sin_part
        imag = imag + tc * sin_part - ts * cos_part
    return real, imag


def transform(source, rows_ref, limit_ref, table_ref, twiddle_ref, store):
    row = lax.broadcasted_iota(jnp.int32, (HALF, 2 * FL), 0)
    lane = lax.broadcasted_iota(jnp.int32, (HALF, 2 * FL), 1)
    group = row // CHUNK
    inner = row - CHUNK * group
    slot = 8 * PIECE * group + 2 * inner + jnp.where(lane >= FL, 1, 0)
    slot = jnp.where(inner == CHUNK - 1, 1 << 20, slot)
    step = ROW_TILES * CHUNK
    tails = []
    for r in range(2):
        inside = slot < limit_ref[2 * source + r, 0:1, :]
        starts = [step * Z_ORDER.index(z) for z in range(r * len(Z_ORDER) // 2, (r + 1) * len(Z_ORDER) // 2)]
        values = jnp.concatenate([rows_ref[start : start + step, :] for start in starts], axis=0)
        values = jnp.where(inside, values.astype(jnp.float32), 0.0)
        values = jnp.concatenate([values[:BASE].T, values[BASE:].T], axis=0).astype(jnp.bfloat16)
        for pair in range(CHIPS // 2):
            sums = combine(values, table_ref, twiddle_ref, source, r, 2 * MAIN * pair, 2 * MAIN)
            for part in range(2):
                for half in range(2):
                    block = sums[part][:, half * MAIN : (half + 1) * MAIN]
                    store(2 * pair + half, (2 * part + r) * FL, block)
        tails.append(combine(values, table_ref, twiddle_ref, source, r, CHIPS * MAIN, CHIPS * TAIL))
    for chip in range(CHIPS):
        lanes = slice(TAIL * chip, TAIL * (chip + 1))
        store(chip, 4 * FL, jnp.concatenate([tails[k % 2][k // 2][:, lanes] for k in range(4)], axis=1))


def own_kernel(rows_ref, limit_ref, table_ref, twiddle_ref, out_ref):
    def store(chip, start, block):
        out_ref[chip, start : start + FL, :] = block

    transform(0, rows_ref, limit_ref, table_ref, twiddle_ref, store)


def other_kernel(own_ref, rows_ref, limit_ref, table_ref, twiddle_ref, out_ref):
    def store(chip, start, block):
        total = own_ref[chip, start : start + FL, :] + block
        out_ref[chip, start : start + FL, :] = total.astype(out_ref.dtype)

    transform(1, rows_ref, limit_ref, table_ref, twiddle_ref, store)


def add_kernel(got_ref, out_ref):
    def total(start, stop):
        sums = got_ref[0, start:stop, :].astype(jnp.float32)
        for chip in range(1, CHIPS):
            sums = sums + got_ref[chip, start:stop, :].astype(jnp.float32)
        return sums

    tail = total(4 * FL, 5 * FL)
    for part in range(2):
        for r in range(2):
            k = 2 * part + r
            main = total(k * FL, (k + 1) * FL)
            both = jnp.concatenate([main, tail[:, k * TAIL : (k + 1) * TAIL]], axis=1)
            out_ref[part, :, r, :] = both


def body(column_state, diffusivity, row_len, lat_rows, wave_order, tile_map):
    f32, bf16 = jnp.float32, jnp.bfloat16
    pos = (2 * lax.axis_index("x") + lax.axis_index("core")).astype(jnp.int32).reshape(1)
    smem = pl.BlockSpec(memory_space=pltpu.SMEM)
    vmem = pl.BlockSpec(memory_space=pltpu.VMEM)
    hbm = pl.BlockSpec(memory_space=pltpu.HBM)
    params = pltpu.CompilerParams(vmem_limit_bytes=VMEM)
    rows = pl.pallas_call(
        solve_kernel,
        out_shape=jax.ShapeDtypeStruct((ROWS, 2 * FL), bf16),
        in_specs=[hbm] * 3,
        out_specs=vmem,
        scratch_shapes=[
            pltpu.VMEM((LEV, NF, TILE_COLS), f32),
            pltpu.VMEM((LEV - 1, TILE_COLS), f32),
            pltpu.VMEM((1, TILE_COLS), jnp.int32),
            pltpu.VMEM((LEV, TILE_COLS), f32),
            pltpu.VMEM((LEV, NF, TILE_COLS), f32),
            pltpu.VMEM((FL, TILE_COLS), f32),
            pltpu.VMEM((2 * ROWS // 128, 8, 128), jnp.int32),
            pltpu.VMEM((ROWS, 2 * FL), f32),
            pltpu.SemaphoreType.DMA((6,)),
        ],
        compiler_params=pltpu.CompilerParams(vmem_limit_bytes=SOLVE_VMEM),
        name="solve",
    )(column_state, diffusivity, tile_map)
    table, twiddle, limit = pl.pallas_call(
        table_kernel,
        out_shape=[
            jax.ShapeDtypeStruct((2, BASE, 2 * SHARE), bf16),
            jax.ShapeDtypeStruct((4, 8, SHARE), f32),
            jax.ShapeDtypeStruct((4, 8, 2 * FL), jnp.int32),
        ],
        in_specs=[smem, smem, smem, vmem],
        out_specs=[vmem, vmem, vmem],
        compiler_params=params,
        cost_estimate=pl.CostEstimate(flops=40_000_000, bytes_accessed=2_200_000, transcendentals=0),
        name="tables",
    )(row_len, lat_rows, pos, wave_order.reshape(PEERS, OWN))
    rows = rows.reshape(SETS, CHUNK // 2, 2, 2 * FL)
    rows = lax.all_to_all(
        rows, "wide", split_axis=0, concat_axis=0, tiled=True, axis_index_groups=[list(ORDER)]
    )
    rows = rows.reshape(ROWS, 2 * FL)
    rows, table, twiddle, limit = lax.optimization_barrier((rows, table, twiddle, limit))
    got = lax.ppermute(rows, "core", [(0, 1), (1, 0)])
    own = pl.pallas_call(
        own_kernel,
        out_shape=jax.ShapeDtypeStruct((CHIPS, 5 * FL, MAIN), f32),
        in_specs=[vmem] * 4,
        out_specs=vmem,
        compiler_params=params,
        cost_estimate=pl.CostEstimate(flops=500_000_000, bytes_accessed=2_000_000, transcendentals=0),
        name="transform_own",
    )(rows, limit, table, twiddle)
    sums = pl.pallas_call(
        other_kernel,
        out_shape=jax.ShapeDtypeStruct((CHIPS, 5 * FL, MAIN), bf16),
        in_specs=[vmem] * 5,
        out_specs=vmem,
        compiler_params=params,
        name="transform_other",
    )(own, got, limit, table, twiddle)
    sums = lax.all_to_all(sums, "x", split_axis=0, concat_axis=0, tiled=True)
    return pl.pallas_call(
        add_kernel,
        out_shape=jax.ShapeDtypeStruct((2, FL, 2, OWN), f32),
        in_specs=[vmem],
        out_specs=vmem,
        compiler_params=params,
        name="add",
    )(sums)


def solution(mesh):
    chips = Mesh(mesh.devices.reshape(SETS, CHIPS, 2), ("wide", "x", "core"))
    columns = ("wide", "x", "core")
    return jax.shard_map(
        body,
        mesh=chips,
        in_specs=(
            P(None, None, columns),
            P(None, columns),
            P(),
            P("wide"),
            P(),
            P(columns, None),
        ),
        out_specs=P(None, None, "wide", ("x", "core")),
        check_vma=False,
    )
```

```python
import math

import jax
import jax.numpy as jnp
from jax import lax
from jax.experimental import pallas as pl
from jax.experimental.pallas import tpu as pltpu
from jax.sharding import Mesh, PartitionSpec as P

LEV = 16
NF = 4
FL = 64
SETS = 64
PIECE = 22
TILE_COLS = 1408
CHUNK = 12
ROWS = SETS * CHUNK
HALF = ROWS // 2
BASE = HALF // 2
OWN = 160
MAIN = 128
TAIL = OWN - MAIN
PEERS = 8
CHIPS = 4
ROW_TILES = 4
Z_ORDER = (8, 7, 9, 6, 10, 5, 11, 4, 12, 3, 13, 2, 14, 1, 15, 0)
ORDER = tuple(z * ROW_TILES + y for z in Z_ORDER for y in range(ROW_TILES))
SHARE = CHIPS * OWN
VMEM = 40 * 1024 * 1024
SOLVE_VMEM = 62 * 1024 * 1024


def lane_gather(values, lanes):
    return jnp.take_along_axis(values, lanes, axis=1, mode="promise_in_bounds")


def solve_kernel(state_hbm, diff_hbm, map_hbm, out_ref, state_ref, diff_ref, map_ref, ratio_ref, value_ref, cols_ref, pick_ref, rows_ref, sems):
    copies = [pltpu.make_async_copy(map_hbm, map_ref, sems.at[0]), pltpu.make_async_copy(diff_hbm, diff_ref, sems.at[1])]
    for part in range(4):
        levels = pl.ds(4 * part, 4)
        copies.append(pltpu.make_async_copy(state_hbm.at[levels], state_ref.at[levels], sems.at[2 + part]))
    for copy in copies:
        copy.start()
    copies[0].wait()
    tiles = ROWS // 128
    for part in range(2):
        for tile in range(tiles):
            place = (lax.broadcasted_iota(jnp.int32, (8, 128), 1) + 128 * tile).astype(jnp.float32)
            chunk = jnp.floor((place + 0.5) * (1.0 / CHUNK))
            inner = place - CHUNK * chunk
            slot = (PIECE * chunk + 2.0 * inner + part).astype(jnp.int32)
            lo_tile = (PIECE * (128 * tile // CHUNK)) // 128
            hi_tile = min(TILE_COLS // 128 - 1, (PIECE * ((128 * tile + 127) // CHUNK) + PIECE - 1) // 128)
            column = jnp.full((8, 128), -1, jnp.int32)
            for k in range(lo_tile, hi_tile + 1):
                entries = jnp.broadcast_to(map_ref[0:1, 128 * k : 128 * (k + 1)], (8, 128))
                found = lane_gather(entries, jnp.bitwise_and(slot, 127))
                column = jnp.where(slot // 128 == k, found, column)
            pick_ref[tiles * part + tile] = jnp.where(inner < PIECE // 2, column, -1)
    copies[1].wait()
    ratio = jnp.zeros((1, TILE_COLS), jnp.float32)
    value = jnp.zeros((NF, TILE_COLS), jnp.float32)
    below = jnp.zeros((1, TILE_COLS), jnp.float32)
    for lev in range(LEV):
        if lev % 4 == 0:
            copies[2 + lev // 4].wait()
        if lev < LEV - 1:
            above = diff_ref[lev : lev + 1, :]
        else:
            above = jnp.zeros((1, TILE_COLS), jnp.float32)
        inverse = 1.0 / (1.0 + below + above + below * ratio)
        ratio = -above * inverse
        value = (state_ref[lev] + below * value) * inverse
        ratio_ref[lev : lev + 1, :] = ratio
        value_ref[lev] = value
        below = above
    solved = value
    cols_ref[(LEV - 1) * NF : LEV * NF, :] = solved
    for lev in range(LEV - 2, -1, -1):
        solved = value_ref[lev] - ratio_ref[lev : lev + 1, :] * solved
        cols_ref[lev * NF : (lev + 1) * NF, :] = solved
    for tile in range(tiles):
        blocks = []
        for part in range(2):
            column = pick_ref[tiles * part + tile]
            lane = jnp.bitwise_and(column, 127)
            source = jnp.right_shift(column, 7)
            hits = [source == k for k in range(TILE_COLS // 128)]
            for first in range(0, FL, 8):
                block = jnp.zeros((8, 128), jnp.float32)
                for k in range(TILE_COLS // 128):
                    found = lane_gather(cols_ref[first : first + 8, 128 * k : 128 * (k + 1)], lane)
                    block = jnp.where(hits[k], found, block)
                blocks.append(block)
        rows_ref[128 * tile : 128 * (tile + 1), :] = jnp.concatenate(blocks, axis=0).T
    step = ROW_TILES * CHUNK
    for place, z in enumerate(Z_ORDER):
        block = rows_ref[step * z : step * (z + 1), :]
        out_ref[step * place : step * (place + 1), :] = block.astype(jnp.bfloat16)


def cos_sin_turns(turns):
    square = turns * turns
    s = jnp.full_like(turns, -(math.pi**11) / math.factorial(11))
    for k, sign in ((9, 1.0), (7, -1.0), (5, 1.0), (3, -1.0), (1, 1.0)):
        s = s * square + sign * math.pi**k / math.factorial(k)
    s = s * turns
    c = jnp.full_like(turns, (math.pi**12) / math.factorial(12))
    for k, sign in ((10, -1.0), (8, 1.0), (6, -1.0), (4, 1.0), (2, -1.0), (0, 1.0)):
        c = c * square + sign * math.pi**k / math.factorial(k)
    return 1.0 - 2.0 * s * s, 2.0 * s * c


def turns_of(product, length, inverse):
    return (product - jnp.floor(product * inverse + 0.5) * length) * inverse


def row_lengths(len_ref, lat_ref, r):
    return len_ref[lat_ref[r]]


def table_kernel(len_ref, lat_ref, pos_ref, wave_ref, table_ref, twiddle_ref, limit_ref):
    core = lax.rem(pos_ref[0], 2)
    rows_of = [wave_ref[pl.ds(2 * chip + core, 1), :] for chip in range(CHIPS)]
    waves = [row[:, 0:MAIN] for row in rows_of] + [row[:, MAIN:OWN] for row in rows_of]
    waves = jnp.concatenate(waves, axis=1).astype(jnp.float32)
    pieces = (pos_ref[0], pos_ref[0] + 1 - 2 * core)
    rows = 8
    for r in range(2):
        count = row_lengths(len_ref, lat_ref, r)
        for source in range(2):
            limit_ref[2 * source + r] = jnp.full((8, 2 * FL), count - PIECE * pieces[source], jnp.int32)
        length = jnp.full((1, SHARE), count, jnp.int32).astype(jnp.float32)
        inverse = 1.0 / length
        scale = lax.rsqrt(length)
        scale = scale * (1.5 - 0.5 * length * scale * scale)

        def some_rows(step, carry):
            first = pl.multiple_of(step * 2 * rows, 2 * rows)
            cosines, sines = [], []
            for part in range(2):
                row = lax.broadcasted_iota(jnp.int32, (rows, SHARE), 0) + (first + part * rows)
                row = row.astype(jnp.float32)
                group = jnp.floor((row + 0.5) * (1.0 / CHUNK))
                slot = 8.0 * PIECE * group + 2.0 * (row - CHUNK * group)
                cosine, sine = cos_sin_turns(turns_of(slot * waves, length, inverse))
                cosines.append(cosine)
                sines.append(-sine)
            table_ref[r, pl.ds(first, 2 * rows), 0:SHARE] = jnp.concatenate(cosines, axis=0).astype(jnp.bfloat16)
            table_ref[r, pl.ds(first, 2 * rows), SHARE:] = jnp.concatenate(sines, axis=0).astype(jnp.bfloat16)
            return carry

        lax.fori_loop(0, BASE // (2 * rows), some_rows, 0)
        item = lax.broadcasted_iota(jnp.int32, (8, SHARE), 0)
        shift = (BASE // CHUNK) * 8 * PIECE * (item // 2 % 2) + item % 2
        shift = shift + PIECE * jnp.where(item < 4, pieces[0], pieces[1])
        cosine, sine = cos_sin_turns(turns_of(shift.astype(jnp.float32) * waves, length, inverse))
        twiddle_ref[2 * r] = cosine * scale
        twiddle_ref[2 * r + 1] = sine * scale


def combine(values, table_ref, twiddle_ref, source, r, first, width):
    lanes = slice(first, first + width)
    cos_all = jnp.dot(values, table_ref[r, :, lanes], preferred_element_type=jnp.float32)
    sin_lanes = slice(SHARE + first, SHARE + first + width)
    sin_all = jnp.dot(values, table_ref[r, :, sin_lanes], preferred_element_type=jnp.float32)
    real = jnp.zeros((FL, width), jnp.float32)
    imag = jnp.zeros((FL, width), jnp.float32)
    for item in range(4):
        cos_part = cos_all[item * FL : (item + 1) * FL]
        sin_part = sin_all[item * FL : (item + 1) * FL]
        k = 4 * source + item
        tc = twiddle_ref[2 * r, k : k + 1, lanes]
        ts = twiddle_ref[2 * r + 1, k : k + 1, lanes]
        real = real + tc * cos_part + ts * sin_part
        imag = imag + tc * sin_part - ts * cos_part
    return real, imag


def transform(source, rows_ref, limit_ref, table_ref, twiddle_ref, store):
    row = lax.broadcasted_iota(jnp.int32, (HALF, 2 * FL), 0)
    lane = lax.broadcasted_iota(jnp.int32, (HALF, 2 * FL), 1)
    group = row // CHUNK
    inner = row - CHUNK * group
    slot = 8 * PIECE * group + 2 * inner + jnp.where(lane >= FL, 1, 0)
    slot = jnp.where(inner == CHUNK - 1, 1 << 20, slot)
    step = ROW_TILES * CHUNK
    tails = []
    for r in range(2):
        inside = slot < limit_ref[2 * source + r, 0:1, :]
        starts = [step * Z_ORDER.index(z) for z in range(r * len(Z_ORDER) // 2, (r + 1) * len(Z_ORDER) // 2)]
        values = jnp.concatenate([rows_ref[start : start + step, :] for start in starts], axis=0)
        values = jnp.where(inside, values.astype(jnp.float32), 0.0)
        values = jnp.concatenate([values[:BASE].T, values[BASE:].T], axis=0).astype(jnp.bfloat16)
        for pair in range(CHIPS // 2):
            sums = combine(values, table_ref, twiddle_ref, source, r, 2 * MAIN * pair, 2 * MAIN)
            for part in range(2):
                for half in range(2):
                    block = sums[part][:, half * MAIN : (half + 1) * MAIN]
                    store(2 * pair + half, (2 * part + r) * FL, block)
        tails.append(combine(values, table_ref, twiddle_ref, source, r, CHIPS * MAIN, CHIPS * TAIL))
    for chip in range(CHIPS):
        lanes = slice(TAIL * chip, TAIL * (chip + 1))
        store(chip, 4 * FL, jnp.concatenate([tails[k % 2][k // 2][:, lanes] for k in range(4)], axis=1))


def own_kernel(rows_ref, limit_ref, table_ref, twiddle_ref, out_ref):
    def store(chip, start, block):
        out_ref[chip, start : start + FL, :] = block

    transform(0, rows_ref, limit_ref, table_ref, twiddle_ref, store)


def other_kernel(own_ref, rows_ref, limit_ref, table_ref, twiddle_ref, out_ref):
    def store(chip, start, block):
        total = own_ref[chip, start : start + FL, :] + block
        out_ref[chip, start : start + FL, :] = total.astype(out_ref.dtype)

    transform(1, rows_ref, limit_ref, table_ref, twiddle_ref, store)


def add_kernel(got_ref, out_ref):
    def total(start, stop):
        sums = got_ref[0, start:stop, :].astype(jnp.float32)
        for chip in range(1, CHIPS):
            sums = sums + got_ref[chip, start:stop, :].astype(jnp.float32)
        return sums

    tail = total(4 * FL, 5 * FL)
    for part in range(2):
        for r in range(2):
            k = 2 * part + r
            main = total(k * FL, (k + 1) * FL)
            both = jnp.concatenate([main, tail[:, k * TAIL : (k + 1) * TAIL]], axis=1)
            out_ref[part, :, r, :] = both


def body(column_state, diffusivity, row_len, lat_rows, wave_order, tile_map):
    f32, bf16 = jnp.float32, jnp.bfloat16
    pos = (2 * lax.axis_index("x") + lax.axis_index("core")).astype(jnp.int32).reshape(1)
    smem = pl.BlockSpec(memory_space=pltpu.SMEM)
    vmem = pl.BlockSpec(memory_space=pltpu.VMEM)
    hbm = pl.BlockSpec(memory_space=pltpu.HBM)
    params = pltpu.CompilerParams(vmem_limit_bytes=VMEM)
    rows = pl.pallas_call(
        solve_kernel,
        out_shape=jax.ShapeDtypeStruct((ROWS, 2 * FL), bf16),
        in_specs=[hbm] * 3,
        out_specs=vmem,
        scratch_shapes=[
            pltpu.VMEM((LEV, NF, TILE_COLS), f32),
            pltpu.VMEM((LEV - 1, TILE_COLS), f32),
            pltpu.VMEM((1, TILE_COLS), jnp.int32),
            pltpu.VMEM((LEV, TILE_COLS), f32),
            pltpu.VMEM((LEV, NF, TILE_COLS), f32),
            pltpu.VMEM((FL, TILE_COLS), f32),
            pltpu.VMEM((2 * ROWS // 128, 8, 128), jnp.int32),
            pltpu.VMEM((ROWS, 2 * FL), f32),
            pltpu.SemaphoreType.DMA((6,)),
        ],
        compiler_params=pltpu.CompilerParams(vmem_limit_bytes=SOLVE_VMEM),
        name="solve",
    )(column_state, diffusivity, tile_map)
    table, twiddle, limit = pl.pallas_call(
        table_kernel,
        out_shape=[
            jax.ShapeDtypeStruct((2, BASE, 2 * SHARE), bf16),
            jax.ShapeDtypeStruct((4, 8, SHARE), f32),
            jax.ShapeDtypeStruct((4, 8, 2 * FL), jnp.int32),
        ],
        in_specs=[smem, smem, smem, vmem],
        out_specs=[vmem, vmem, vmem],
        compiler_params=params,
        cost_estimate=pl.CostEstimate(flops=40_000_000, bytes_accessed=2_200_000, transcendentals=0),
        name="tables",
    )(row_len, lat_rows, pos, wave_order.reshape(PEERS, OWN))
    rows = rows.reshape(SETS, CHUNK // 2, 2, 2 * FL)
    rows = lax.all_to_all(
        rows, "wide", split_axis=0, concat_axis=0, tiled=True, axis_index_groups=[list(ORDER)]
    )
    rows = rows.reshape(ROWS, 2 * FL)
    rows, table, twiddle, limit = lax.optimization_barrier((rows, table, twiddle, limit))
    got = lax.ppermute(rows, "core", [(0, 1), (1, 0)])
    own = pl.pallas_call(
        own_kernel,
        out_shape=jax.ShapeDtypeStruct((CHIPS, 5 * FL, MAIN), f32),
        in_specs=[vmem] * 4,
        out_specs=vmem,
        compiler_params=params,
        cost_estimate=pl.CostEstimate(flops=500_000_000, bytes_accessed=2_000_000, transcendentals=0),
        name="transform_own",
    )(rows, limit, table, twiddle)
    sums = pl.pallas_call(
        other_kernel,
        out_shape=jax.ShapeDtypeStruct((CHIPS, 5 * FL, MAIN), bf16),
        in_specs=[vmem] * 5,
        out_specs=vmem,
        compiler_params=params,
        name="transform_other",
    )(own, got, limit, table, twiddle)
    sums = lax.all_to_all(sums, "x", split_axis=0, concat_axis=0, tiled=True)
    return pl.pallas_call(
        add_kernel,
        out_shape=jax.ShapeDtypeStruct((2, FL, 2, OWN), f32),
        in_specs=[vmem],
        out_specs=vmem,
        compiler_params=params,
        name="add",
    )(sums)


def solution(mesh):
    chips = Mesh(mesh.devices.reshape(SETS, CHIPS, 2), ("wide", "x", "core"))
    columns = ("wide", "x", "core")
    return jax.shard_map(
        body,
        mesh=chips,
        in_specs=(
            P(None, None, columns),
            P(None, columns),
            P(),
            P("wide"),
            P(),
            P(columns, None),
        ),
        out_specs=P(None, None, "wide", ("x", "core")),
        check_vma=False,
    )
```

```python
import math

import jax
import jax.numpy as jnp
from jax import lax
from jax.experimental import pallas as pl
from jax.experimental.pallas import tpu as pltpu
from jax.sharding import Mesh, PartitionSpec as P

LEV = 16
NF = 4
FL = 64
SETS = 64
PIECE = 22
TILE_COLS = 1408
CHUNK = 12
ROWS = SETS * CHUNK
HALF = ROWS // 2
BASE = HALF // 2
OWN = 160
MAIN = 128
TAIL = OWN - MAIN
PEERS = 8
CHIPS = 4
X_ORDER = (2, 1, 3, 0)
ROW_TILES = 4
Z_ORDER = (10, 9, 11, 8, 12, 7, 13, 6, 14, 5, 15, 4, 0, 3, 1, 2)
Y_FIRST = 2
ORDER = tuple(z * ROW_TILES + (Y_FIRST + y) % ROW_TILES for z in Z_ORDER for y in range(ROW_TILES))
SHARE = CHIPS * OWN
VMEM = 40 * 1024 * 1024
SOLVE_VMEM = 62 * 1024 * 1024


def lane_gather(values, lanes):
    return jnp.take_along_axis(values, lanes, axis=1, mode="promise_in_bounds")


def tile_of(listed):
    z = jnp.floor((listed + 0.5) * (1.0 / ROW_TILES))
    y = listed - ROW_TILES * z + Y_FIRST
    return ROW_TILES * z + jnp.where(y >= ROW_TILES, y - ROW_TILES, y)


def solve_kernel(state_hbm, diff_hbm, map_hbm, out_ref, state_ref, diff_ref, map_ref, ratio_ref, value_ref, cols_ref, pick_ref, rows_ref, sems):
    copies = [pltpu.make_async_copy(map_hbm, map_ref, sems.at[0]), pltpu.make_async_copy(diff_hbm, diff_ref, sems.at[1])]
    for part in range(4):
        levels = pl.ds(4 * part, 4)
        copies.append(pltpu.make_async_copy(state_hbm.at[levels], state_ref.at[levels], sems.at[2 + part]))
    for copy in copies:
        copy.start()
    copies[0].wait()
    tiles = ROWS // 128
    for part in range(2):
        for tile in range(tiles):
            place = (lax.broadcasted_iota(jnp.int32, (8, 128), 1) + 128 * tile).astype(jnp.float32)
            chunk = jnp.floor((place + 0.5) * (1.0 / CHUNK))
            inner = place - CHUNK * chunk
            slot = (PIECE * tile_of(chunk) + 2.0 * inner + part).astype(jnp.int32)
            span = PIECE * ROW_TILES
            step = CHUNK * ROW_TILES
            lo_tile = (span * (128 * tile // step)) // 128
            hi_tile = min(TILE_COLS // 128 - 1, (span * ((128 * tile + 127) // step + 1) - 1) // 128)
            column = jnp.full((8, 128), -1, jnp.int32)
            for k in range(lo_tile, hi_tile + 1):
                entries = jnp.broadcast_to(map_ref[0:1, 128 * k : 128 * (k + 1)], (8, 128))
                found = lane_gather(entries, jnp.bitwise_and(slot, 127))
                column = jnp.where(slot // 128 == k, found, column)
            pick_ref[tiles * part + tile] = jnp.where(inner < PIECE // 2, column, -1)
    copies[1].wait()
    ratio = jnp.zeros((1, TILE_COLS), jnp.float32)
    value = jnp.zeros((NF, TILE_COLS), jnp.float32)
    below = jnp.zeros((1, TILE_COLS), jnp.float32)
    for lev in range(LEV):
        if lev % 4 == 0:
            copies[2 + lev // 4].wait()
        if lev < LEV - 1:
            above = diff_ref[lev : lev + 1, :]
        else:
            above = jnp.zeros((1, TILE_COLS), jnp.float32)
        inverse = 1.0 / (1.0 + below + above + below * ratio)
        ratio = -above * inverse
        value = (state_ref[lev] + below * value) * inverse
        ratio_ref[lev : lev + 1, :] = ratio
        value_ref[lev] = value
        below = above
    solved = value
    cols_ref[(LEV - 1) * NF : LEV * NF, :] = solved
    for lev in range(LEV - 2, -1, -1):
        solved = value_ref[lev] - ratio_ref[lev : lev + 1, :] * solved
        cols_ref[lev * NF : (lev + 1) * NF, :] = solved
    for tile in range(tiles):
        blocks = []
        for part in range(2):
            column = pick_ref[tiles * part + tile]
            lane = jnp.bitwise_and(column, 127)
            source = jnp.right_shift(column, 7)
            hits = [source == k for k in range(TILE_COLS // 128)]
            for first in range(0, FL, 8):
                block = jnp.zeros((8, 128), jnp.float32)
                for k in range(TILE_COLS // 128):
                    found = lane_gather(cols_ref[first : first + 8, 128 * k : 128 * (k + 1)], lane)
                    block = jnp.where(hits[k], found, block)
                blocks.append(block)
        rows_ref[128 * tile : 128 * (tile + 1), :] = jnp.concatenate(blocks, axis=0).T
    step = ROW_TILES * CHUNK
    for place, z in enumerate(Z_ORDER):
        block = rows_ref[step * z : step * (z + 1), :]
        out_ref[step * place : step * (place + 1), :] = block.astype(jnp.bfloat16)


def cos_sin_turns(turns):
    square = turns * turns
    s = jnp.full_like(turns, -(math.pi**11) / math.factorial(11))
    for k, sign in ((9, 1.0), (7, -1.0), (5, 1.0), (3, -1.0), (1, 1.0)):
        s = s * square + sign * math.pi**k / math.factorial(k)
    s = s * turns
    c = jnp.full_like(turns, (math.pi**12) / math.factorial(12))
    for k, sign in ((10, -1.0), (8, 1.0), (6, -1.0), (4, 1.0), (2, -1.0), (0, 1.0)):
        c = c * square + sign * math.pi**k / math.factorial(k)
    return 1.0 - 2.0 * s * s, 2.0 * s * c


def turns_of(product, length, inverse):
    return (product - jnp.floor(product * inverse + 0.5) * length) * inverse


def row_lengths(len_ref, lat_ref, r):
    return len_ref[lat_ref[r]]


def table_kernel(len_ref, lat_ref, pos_ref, wave_ref, table_ref, twiddle_ref, limit_ref):
    core = lax.rem(pos_ref[0], 2)
    rows_of = [wave_ref[pl.ds(2 * chip + core, 1), :] for chip in range(CHIPS)]
    waves = [row[:, 0:MAIN] for row in rows_of] + [row[:, MAIN:OWN] for row in rows_of]
    waves = jnp.concatenate(waves, axis=1).astype(jnp.float32)
    pieces = (pos_ref[0], pos_ref[0] + 1 - 2 * core)
    rows = 8
    for r in range(2):
        count = row_lengths(len_ref, lat_ref, r)
        for source in range(2):
            limit_ref[2 * source + r] = jnp.full((8, 2 * FL), count - PIECE * pieces[source], jnp.int32)
        length = jnp.full((1, SHARE), count, jnp.int32).astype(jnp.float32)
        inverse = 1.0 / length
        scale = lax.rsqrt(length)
        scale = scale * (1.5 - 0.5 * length * scale * scale)

        def some_rows(step, carry):
            first = pl.multiple_of(step * 2 * rows, 2 * rows)
            cosines, sines = [], []
            for part in range(2):
                row = lax.broadcasted_iota(jnp.int32, (rows, SHARE), 0) + (first + part * rows)
                row = row.astype(jnp.float32)
                group = jnp.floor((row + 0.5) * (1.0 / CHUNK))
                slot = 8.0 * PIECE * tile_of(group) + 2.0 * (row - CHUNK * group)
                cosine, sine = cos_sin_turns(turns_of(slot * waves, length, inverse))
                cosines.append(cosine)
                sines.append(-sine)
            table_ref[r, pl.ds(first, 2 * rows), 0:SHARE] = jnp.concatenate(cosines, axis=0).astype(jnp.bfloat16)
            table_ref[r, pl.ds(first, 2 * rows), SHARE:] = jnp.concatenate(sines, axis=0).astype(jnp.bfloat16)
            return carry

        lax.fori_loop(0, BASE // (2 * rows), some_rows, 0)
        item = lax.broadcasted_iota(jnp.int32, (8, SHARE), 0)
        shift = (BASE // CHUNK) * 8 * PIECE * (item // 2 % 2) + item % 2
        shift = shift + PIECE * jnp.where(item < 4, pieces[0], pieces[1])
        cosine, sine = cos_sin_turns(turns_of(shift.astype(jnp.float32) * waves, length, inverse))
        twiddle_ref[2 * r] = cosine * scale
        twiddle_ref[2 * r + 1] = sine * scale


def combine(values, table_ref, twiddle_ref, source, r, first, width):
    lanes = slice(first, first + width)
    cos_all = jnp.dot(values, table_ref[r, :, lanes], preferred_element_type=jnp.float32)
    sin_lanes = slice(SHARE + first, SHARE + first + width)
    sin_all = jnp.dot(values, table_ref[r, :, sin_lanes], preferred_element_type=jnp.float32)
    real = jnp.zeros((FL, width), jnp.float32)
    imag = jnp.zeros((FL, width), jnp.float32)
    for item in range(4):
        cos_part = cos_all[item * FL : (item + 1) * FL]
        sin_part = sin_all[item * FL : (item + 1) * FL]
        k = 4 * source + item
        tc = twiddle_ref[2 * r, k : k + 1, lanes]
        ts = twiddle_ref[2 * r + 1, k : k + 1, lanes]
        real = real + tc * cos_part + ts * sin_part
        imag = imag + tc * sin_part - ts * cos_part
    return real, imag


def transform(source, rows_ref, limit_ref, table_ref, twiddle_ref, store):
    row = lax.broadcasted_iota(jnp.int32, (HALF, 2 * FL), 0)
    lane = lax.broadcasted_iota(jnp.int32, (HALF, 2 * FL), 1)
    group = row // CHUNK
    inner = row - CHUNK * group
    tile = group // ROW_TILES * ROW_TILES + (group + Y_FIRST) % ROW_TILES
    slot = 8 * PIECE * tile + 2 * inner + jnp.where(lane >= FL, 1, 0)
    slot = jnp.where(inner == CHUNK - 1, 1 << 20, slot)
    step = ROW_TILES * CHUNK
    tails = []
    for r in range(2):
        inside = slot < limit_ref[2 * source + r, 0:1, :]
        starts = [step * Z_ORDER.index(z) for z in range(r * len(Z_ORDER) // 2, (r + 1) * len(Z_ORDER) // 2)]
        values = jnp.concatenate([rows_ref[start : start + step, :] for start in starts], axis=0)
        values = jnp.where(inside, values.astype(jnp.float32), 0.0)
        values = jnp.concatenate([values[:BASE].T, values[BASE:].T], axis=0).astype(jnp.bfloat16)
        for pair in range(CHIPS // 2):
            sums = combine(values, table_ref, twiddle_ref, source, r, 2 * MAIN * pair, 2 * MAIN)
            for part in range(2):
                for half in range(2):
                    block = sums[part][:, half * MAIN : (half + 1) * MAIN]
                    store(2 * pair + half, (2 * part + r) * FL, block)
        tails.append(combine(values, table_ref, twiddle_ref, source, r, CHIPS * MAIN, CHIPS * TAIL))
    for chip in range(CHIPS):
        lanes = slice(TAIL * chip, TAIL * (chip + 1))
        store(chip, 4 * FL, jnp.concatenate([tails[k % 2][k // 2][:, lanes] for k in range(4)], axis=1))


def own_kernel(rows_ref, limit_ref, table_ref, twiddle_ref, out_ref):
    def store(chip, start, block):
        out_ref[chip, start : start + FL, :] = block

    transform(0, rows_ref, limit_ref, table_ref, twiddle_ref, store)


def other_kernel(own_ref, rows_ref, limit_ref, table_ref, twiddle_ref, out_ref):
    def store(chip, start, block):
        total = own_ref[chip, start : start + FL, :] + block
        out_ref[X_ORDER.index(chip), start : start + FL, :] = total.astype(out_ref.dtype)

    transform(1, rows_ref, limit_ref, table_ref, twiddle_ref, store)


def add_kernel(got_ref, out_ref):
    def total(start, stop):
        sums = got_ref[0, start:stop, :].astype(jnp.float32)
        for chip in range(1, CHIPS):
            sums = sums + got_ref[chip, start:stop, :].astype(jnp.float32)
        return sums

    tail = total(4 * FL, 5 * FL)
    for part in range(2):
        for r in range(2):
            k = 2 * part + r
            main = total(k * FL, (k + 1) * FL)
            both = jnp.concatenate([main, tail[:, k * TAIL : (k + 1) * TAIL]], axis=1)
            out_ref[part, :, r, :] = both


def body(column_state, diffusivity, row_len, lat_rows, wave_order, tile_map):
    f32, bf16 = jnp.float32, jnp.bfloat16
    pos = (2 * lax.axis_index("x") + lax.axis_index("core")).astype(jnp.int32).reshape(1)
    smem = pl.BlockSpec(memory_space=pltpu.SMEM)
    vmem = pl.BlockSpec(memory_space=pltpu.VMEM)
    hbm = pl.BlockSpec(memory_space=pltpu.HBM)
    params = pltpu.CompilerParams(vmem_limit_bytes=VMEM)
    rows = pl.pallas_call(
        solve_kernel,
        out_shape=jax.ShapeDtypeStruct((ROWS, 2 * FL), bf16),
        in_specs=[hbm] * 3,
        out_specs=vmem,
        scratch_shapes=[
            pltpu.VMEM((LEV, NF, TILE_COLS), f32),
            pltpu.VMEM((LEV - 1, TILE_COLS), f32),
            pltpu.VMEM((1, TILE_COLS), jnp.int32),
            pltpu.VMEM((LEV, TILE_COLS), f32),
            pltpu.VMEM((LEV, NF, TILE_COLS), f32),
            pltpu.VMEM((FL, TILE_COLS), f32),
            pltpu.VMEM((2 * ROWS // 128, 8, 128), jnp.int32),
            pltpu.VMEM((ROWS, 2 * FL), f32),
            pltpu.SemaphoreType.DMA((6,)),
        ],
        compiler_params=pltpu.CompilerParams(vmem_limit_bytes=SOLVE_VMEM),
        name="solve",
    )(column_state, diffusivity, tile_map)
    table, twiddle, limit = pl.pallas_call(
        table_kernel,
        out_shape=[
            jax.ShapeDtypeStruct((2, BASE, 2 * SHARE), bf16),
            jax.ShapeDtypeStruct((4, 8, SHARE), f32),
            jax.ShapeDtypeStruct((4, 8, 2 * FL), jnp.int32),
        ],
        in_specs=[smem, smem, smem, vmem],
        out_specs=[vmem, vmem, vmem],
        compiler_params=params,
        cost_estimate=pl.CostEstimate(flops=40_000_000, bytes_accessed=2_200_000, transcendentals=0),
        name="tables",
    )(row_len, lat_rows, pos, wave_order.reshape(PEERS, OWN))
    rows = rows.reshape(SETS, CHUNK // 2, 2, 2 * FL)
    rows = lax.all_to_all(
        rows, "wide", split_axis=0, concat_axis=0, tiled=True, axis_index_groups=[list(ORDER)]
    )
    rows = rows.reshape(ROWS, 2 * FL)
    rows, table, twiddle, limit = lax.optimization_barrier((rows, table, twiddle, limit))
    got = lax.ppermute(rows, "core", [(0, 1), (1, 0)])
    own = pl.pallas_call(
        own_kernel,
        out_shape=jax.ShapeDtypeStruct((CHIPS, 5 * FL, MAIN), f32),
        in_specs=[vmem] * 4,
        out_specs=vmem,
        compiler_params=params,
        cost_estimate=pl.CostEstimate(flops=500_000_000, bytes_accessed=2_000_000, transcendentals=0),
        name="transform_own",
    )(rows, limit, table, twiddle)
    sums = pl.pallas_call(
        other_kernel,
        out_shape=jax.ShapeDtypeStruct((CHIPS, 5 * FL, MAIN), bf16),
        in_specs=[vmem] * 5,
        out_specs=vmem,
        compiler_params=params,
        name="transform_other",
    )(own, got, limit, table, twiddle)
    sums = lax.all_to_all(
        sums, "x", split_axis=0, concat_axis=0, tiled=True, axis_index_groups=[list(X_ORDER)]
    )
    return pl.pallas_call(
        add_kernel,
        out_shape=jax.ShapeDtypeStruct((2, FL, 2, OWN), f32),
        in_specs=[vmem],
        out_specs=vmem,
        compiler_params=params,
        name="add",
    )(sums)


def solution(mesh):
    chips = Mesh(mesh.devices.reshape(SETS, CHIPS, 2), ("wide", "x", "core"))
    columns = ("wide", "x", "core")
    return jax.shard_map(
        body,
        mesh=chips,
        in_specs=(
            P(None, None, columns),
            P(None, columns),
            P(),
            P("wide"),
            P(),
            P(columns, None),
        ),
        out_specs=P(None, None, "wide", ("x", "core")),
        check_vma=False,
    )
```

```python
import math

import jax
import jax.numpy as jnp
from jax import lax
from jax.experimental import pallas as pl
from jax.experimental.pallas import tpu as pltpu
from jax.sharding import Mesh, PartitionSpec as P

LEV = 16
NF = 4
FL = 64
SETS = 64
PIECE = 22
TILE_COLS = 1408
CHUNK = 12
ROWS = SETS * CHUNK
HALF = ROWS // 2
BASE = HALF // 2
OWN = 160
MAIN = 128
TAIL = OWN - MAIN
PEERS = 8
CHIPS = 4
X_ORDER = (2, 1, 3, 0)
ROW_TILES = 4
Z_ORDER = (10, 9, 11, 8, 12, 7, 13, 6, 14, 5, 15, 4, 0, 3, 1, 2)
Y_FIRST = 2
ORDER = tuple(z * ROW_TILES + (Y_FIRST + y) % ROW_TILES for z in Z_ORDER for y in range(ROW_TILES))
SHARE = CHIPS * OWN
VMEM = 40 * 1024 * 1024
SOLVE_VMEM = 62 * 1024 * 1024


def lane_gather(values, lanes):
    return jnp.take_along_axis(values, lanes, axis=1, mode="promise_in_bounds")


def tile_of(listed):
    z = jnp.floor((listed + 0.5) * (1.0 / ROW_TILES))
    y = listed - ROW_TILES * z + Y_FIRST
    return ROW_TILES * z + jnp.where(y >= ROW_TILES, y - ROW_TILES, y)


def solve_kernel(state_hbm, diff_hbm, map_hbm, out_ref, state_ref, diff_ref, map_ref, ratio_ref, value_ref, cols_ref, pick_ref, rows_ref, sent_ref, sems, out_sems):
    copies = [pltpu.make_async_copy(map_hbm, map_ref, sems.at[0]), pltpu.make_async_copy(diff_hbm, diff_ref, sems.at[1])]
    for part in range(4):
        levels = pl.ds(4 * part, 4)
        copies.append(pltpu.make_async_copy(state_hbm.at[levels], state_ref.at[levels], sems.at[2 + part]))
    for copy in copies:
        copy.start()
    copies[0].wait()
    tiles = ROWS // 128
    for part in range(2):
        for tile in range(tiles):
            place = (lax.broadcasted_iota(jnp.int32, (8, 128), 1) + 128 * tile).astype(jnp.float32)
            chunk = jnp.floor((place + 0.5) * (1.0 / CHUNK))
            inner = place - CHUNK * chunk
            slot = (PIECE * tile_of(chunk) + 2.0 * inner + part).astype(jnp.int32)
            span = PIECE * ROW_TILES
            step = CHUNK * ROW_TILES
            lo_tile = (span * (128 * tile // step)) // 128
            hi_tile = min(TILE_COLS // 128 - 1, (span * ((128 * tile + 127) // step + 1) - 1) // 128)
            column = jnp.full((8, 128), -1, jnp.int32)
            for k in range(lo_tile, hi_tile + 1):
                entries = jnp.broadcast_to(map_ref[0:1, 128 * k : 128 * (k + 1)], (8, 128))
                found = lane_gather(entries, jnp.bitwise_and(slot, 127))
                column = jnp.where(slot // 128 == k, found, column)
            pick_ref[tiles * part + tile] = jnp.where(inner < PIECE // 2, column, -1)
    copies[1].wait()
    ratio = jnp.zeros((1, TILE_COLS), jnp.float32)
    value = jnp.zeros((NF, TILE_COLS), jnp.float32)
    below = jnp.zeros((1, TILE_COLS), jnp.float32)
    for lev in range(LEV):
        if lev % 4 == 0:
            copies[2 + lev // 4].wait()
        if lev < LEV - 1:
            above = diff_ref[lev : lev + 1, :]
        else:
            above = jnp.zeros((1, TILE_COLS), jnp.float32)
        inverse = 1.0 / (1.0 + below + above + below * ratio)
        ratio = -above * inverse
        value = (state_ref[lev] + below * value) * inverse
        ratio_ref[lev : lev + 1, :] = ratio
        value_ref[lev] = value
        below = above
    solved = value
    cols_ref[(LEV - 1) * NF : LEV * NF, :] = solved
    for lev in range(LEV - 2, -1, -1):
        solved = value_ref[lev] - ratio_ref[lev : lev + 1, :] * solved
        cols_ref[lev * NF : (lev + 1) * NF, :] = solved
    sent = []
    for tile in range(tiles):
        blocks = []
        for part in range(2):
            column = pick_ref[tiles * part + tile]
            lane = jnp.bitwise_and(column, 127)
            source = jnp.right_shift(column, 7)
            hits = [source == k for k in range(TILE_COLS // 128)]
            for first in range(0, FL, 8):
                block = jnp.zeros((8, 128), jnp.float32)
                for k in range(TILE_COLS // 128):
                    found = lane_gather(cols_ref[first : first + 8, 128 * k : 128 * (k + 1)], lane)
                    block = jnp.where(hits[k], found, block)
                blocks.append(block)
        rows_ref[128 * tile : 128 * (tile + 1), :] = jnp.concatenate(blocks, axis=0).T
        step = ROW_TILES * CHUNK
        for z in range(128 * tile // step, 128 * (tile + 1) // step):
            place = pl.ds(step * Z_ORDER.index(z), step)
            sent_ref[place, :] = rows_ref[step * z : step * (z + 1), :].astype(jnp.bfloat16)
            copy = pltpu.make_async_copy(sent_ref.at[place], out_ref.at[place], out_sems.at[z])
            copy.start()
            sent.append(copy)
    for copy in sent:
        copy.wait()


def cos_sin_turns(turns):
    square = turns * turns
    s = jnp.full_like(turns, -(math.pi**11) / math.factorial(11))
    for k, sign in ((9, 1.0), (7, -1.0), (5, 1.0), (3, -1.0), (1, 1.0)):
        s = s * square + sign * math.pi**k / math.factorial(k)
    s = s * turns
    c = jnp.full_like(turns, (math.pi**12) / math.factorial(12))
    for k, sign in ((10, -1.0), (8, 1.0), (6, -1.0), (4, 1.0), (2, -1.0), (0, 1.0)):
        c = c * square + sign * math.pi**k / math.factorial(k)
    return 1.0 - 2.0 * s * s, 2.0 * s * c


def turns_of(product, length, inverse):
    return (product - jnp.floor(product * inverse + 0.5) * length) * inverse


def row_lengths(len_ref, lat_ref, r):
    return len_ref[lat_ref[r]]


def table_kernel(len_ref, lat_ref, pos_ref, wave_ref, table_ref, twiddle_ref, limit_ref):
    core = lax.rem(pos_ref[0], 2)
    rows_of = [wave_ref[pl.ds(2 * chip + core, 1), :] for chip in range(CHIPS)]
    waves = [row[:, 0:MAIN] for row in rows_of] + [row[:, MAIN:OWN] for row in rows_of]
    waves = jnp.concatenate(waves, axis=1).astype(jnp.float32)
    pieces = (pos_ref[0], pos_ref[0] + 1 - 2 * core)
    rows = 8
    for r in range(2):
        count = row_lengths(len_ref, lat_ref, r)
        for source in range(2):
            limit_ref[2 * source + r] = jnp.full((8, 2 * FL), count - PIECE * pieces[source], jnp.int32)
        length = jnp.full((1, SHARE), count, jnp.int32).astype(jnp.float32)
        inverse = 1.0 / length
        scale = lax.rsqrt(length)
        scale = scale * (1.5 - 0.5 * length * scale * scale)

        def some_rows(step, carry):
            first = pl.multiple_of(step * 2 * rows, 2 * rows)
            cosines, sines = [], []
            for part in range(2):
                row = lax.broadcasted_iota(jnp.int32, (rows, SHARE), 0) + (first + part * rows)
                row = row.astype(jnp.float32)
                group = jnp.floor((row + 0.5) * (1.0 / CHUNK))
                slot = 8.0 * PIECE * tile_of(group) + 2.0 * (row - CHUNK * group)
                cosine, sine = cos_sin_turns(turns_of(slot * waves, length, inverse))
                cosines.append(cosine)
                sines.append(-sine)
            table_ref[r, pl.ds(first, 2 * rows), 0:SHARE] = jnp.concatenate(cosines, axis=0).astype(jnp.bfloat16)
            table_ref[r, pl.ds(first, 2 * rows), SHARE:] = jnp.concatenate(sines, axis=0).astype(jnp.bfloat16)
            return carry

        lax.fori_loop(0, BASE // (2 * rows), some_rows, 0)
        item = lax.broadcasted_iota(jnp.int32, (8, SHARE), 0)
        shift = (BASE // CHUNK) * 8 * PIECE * (item // 2 % 2) + item % 2
        shift = shift + PIECE * jnp.where(item < 4, pieces[0], pieces[1])
        cosine, sine = cos_sin_turns(turns_of(shift.astype(jnp.float32) * waves, length, inverse))
        twiddle_ref[2 * r] = cosine * scale
        twiddle_ref[2 * r + 1] = sine * scale


def combine(values, table_ref, twiddle_ref, source, r, first, width):
    lanes = slice(first, first + width)
    cos_all = jnp.dot(values, table_ref[r, :, lanes], preferred_element_type=jnp.float32)
    sin_lanes = slice(SHARE + first, SHARE + first + width)
    sin_all = jnp.dot(values, table_ref[r, :, sin_lanes], preferred_element_type=jnp.float32)
    real = jnp.zeros((FL, width), jnp.float32)
    imag = jnp.zeros((FL, width), jnp.float32)
    for item in range(4):
        cos_part = cos_all[item * FL : (item + 1) * FL]
        sin_part = sin_all[item * FL : (item + 1) * FL]
        k = 4 * source + item
        tc = twiddle_ref[2 * r, k : k + 1, lanes]
        ts = twiddle_ref[2 * r + 1, k : k + 1, lanes]
        real = real + tc * cos_part + ts * sin_part
        imag = imag + tc * sin_part - ts * cos_part
    return real, imag


def transform(source, rows_ref, limit_ref, table_ref, twiddle_ref, store):
    row = lax.broadcasted_iota(jnp.int32, (HALF, 2 * FL), 0)
    lane = lax.broadcasted_iota(jnp.int32, (HALF, 2 * FL), 1)
    group = row // CHUNK
    inner = row - CHUNK * group
    tile = group // ROW_TILES * ROW_TILES + (group + Y_FIRST) % ROW_TILES
    slot = 8 * PIECE * tile + 2 * inner + jnp.where(lane >= FL, 1, 0)
    slot = jnp.where(inner == CHUNK - 1, 1 << 20, slot)
    step = ROW_TILES * CHUNK
    tails = []
    for r in range(2):
        inside = slot < limit_ref[2 * source + r, 0:1, :]
        starts = [step * Z_ORDER.index(z) for z in range(r * len(Z_ORDER) // 2, (r + 1) * len(Z_ORDER) // 2)]
        values = jnp.concatenate([rows_ref[start : start + step, :] for start in starts], axis=0)
        values = jnp.where(inside, values.astype(jnp.float32), 0.0)
        values = jnp.concatenate([values[:BASE].T, values[BASE:].T], axis=0).astype(jnp.bfloat16)
        for pair in range(CHIPS // 2):
            sums = combine(values, table_ref, twiddle_ref, source, r, 2 * MAIN * pair, 2 * MAIN)
            for part in range(2):
                for half in range(2):
                    block = sums[part][:, half * MAIN : (half + 1) * MAIN]
                    store(2 * pair + half, (2 * part + r) * FL, block)
        tails.append(combine(values, table_ref, twiddle_ref, source, r, CHIPS * MAIN, CHIPS * TAIL))
    for chip in range(CHIPS):
        lanes = slice(TAIL * chip, TAIL * (chip + 1))
        store(chip, 4 * FL, jnp.concatenate([tails[k % 2][k // 2][:, lanes] for k in range(4)], axis=1))


def own_kernel(rows_ref, limit_ref, table_ref, twiddle_ref, out_ref):
    def store(chip, start, block):
        out_ref[chip, start : start + FL, :] = block

    transform(0, rows_ref, limit_ref, table_ref, twiddle_ref, store)


def other_kernel(own_ref, rows_ref, limit_ref, table_ref, twiddle_ref, out_ref):
    def store(chip, start, block):
        total = own_ref[chip, start : start + FL, :] + block
        out_ref[X_ORDER.index(chip), start : start + FL, :] = total.astype(out_ref.dtype)

    transform(1, rows_ref, limit_ref, table_ref, twiddle_ref, store)


def add_kernel(got_ref, out_ref):
    def total(start, stop):
        sums = got_ref[0, start:stop, :].astype(jnp.float32)
        for chip in range(1, CHIPS):
            sums = sums + got_ref[chip, start:stop, :].astype(jnp.float32)
        return sums

    tail = total(4 * FL, 5 * FL)
    for part in range(2):
        for r in range(2):
            k = 2 * part + r
            main = total(k * FL, (k + 1) * FL)
            both = jnp.concatenate([main, tail[:, k * TAIL : (k + 1) * TAIL]], axis=1)
            out_ref[part, :, r, :] = both


def body(column_state, diffusivity, row_len, lat_rows, wave_order, tile_map):
    f32, bf16 = jnp.float32, jnp.bfloat16
    pos = (2 * lax.axis_index("x") + lax.axis_index("core")).astype(jnp.int32).reshape(1)
    smem = pl.BlockSpec(memory_space=pltpu.SMEM)
    vmem = pl.BlockSpec(memory_space=pltpu.VMEM)
    hbm = pl.BlockSpec(memory_space=pltpu.HBM)
    params = pltpu.CompilerParams(vmem_limit_bytes=VMEM)
    rows = pl.pallas_call(
        solve_kernel,
        out_shape=jax.ShapeDtypeStruct((ROWS, 2 * FL), bf16),
        in_specs=[hbm] * 3,
        out_specs=hbm,
        scratch_shapes=[
            pltpu.VMEM((LEV, NF, TILE_COLS), f32),
            pltpu.VMEM((LEV - 1, TILE_COLS), f32),
            pltpu.VMEM((1, TILE_COLS), jnp.int32),
            pltpu.VMEM((LEV, TILE_COLS), f32),
            pltpu.VMEM((LEV, NF, TILE_COLS), f32),
            pltpu.VMEM((FL, TILE_COLS), f32),
            pltpu.VMEM((2 * ROWS // 128, 8, 128), jnp.int32),
            pltpu.VMEM((ROWS, 2 * FL), f32),
            pltpu.VMEM((ROWS, 2 * FL), bf16),
            pltpu.SemaphoreType.DMA((6,)),
            pltpu.SemaphoreType.DMA((len(Z_ORDER),)),
        ],
        compiler_params=pltpu.CompilerParams(vmem_limit_bytes=SOLVE_VMEM),
        name="solve",
    )(column_state, diffusivity, tile_map)
    table, twiddle, limit = pl.pallas_call(
        table_kernel,
        out_shape=[
            jax.ShapeDtypeStruct((2, BASE, 2 * SHARE), bf16),
            jax.ShapeDtypeStruct((4, 8, SHARE), f32),
            jax.ShapeDtypeStruct((4, 8, 2 * FL), jnp.int32),
        ],
        in_specs=[smem, smem, smem, vmem],
        out_specs=[vmem, vmem, vmem],
        compiler_params=params,
        cost_estimate=pl.CostEstimate(flops=40_000_000, bytes_accessed=2_200_000, transcendentals=0),
        name="tables",
    )(row_len, lat_rows, pos, wave_order.reshape(PEERS, OWN))
    rows = rows.reshape(SETS, CHUNK // 2, 2, 2 * FL)
    rows = lax.all_to_all(
        rows, "wide", split_axis=0, concat_axis=0, tiled=True, axis_index_groups=[list(ORDER)]
    )
    rows = rows.reshape(ROWS, 2 * FL)
    rows, table, twiddle, limit = lax.optimization_barrier((rows, table, twiddle, limit))
    got = lax.ppermute(rows, "core", [(0, 1), (1, 0)])
    own = pl.pallas_call(
        own_kernel,
        out_shape=jax.ShapeDtypeStruct((CHIPS, 5 * FL, MAIN), f32),
        in_specs=[vmem] * 4,
        out_specs=vmem,
        compiler_params=params,
        cost_estimate=pl.CostEstimate(flops=500_000_000, bytes_accessed=2_000_000, transcendentals=0),
        name="transform_own",
    )(rows, limit, table, twiddle)
    sums = pl.pallas_call(
        other_kernel,
        out_shape=jax.ShapeDtypeStruct((CHIPS, 5 * FL, MAIN), bf16),
        in_specs=[vmem] * 5,
        out_specs=vmem,
        compiler_params=params,
        name="transform_other",
    )(own, got, limit, table, twiddle)
    sums = lax.all_to_all(
        sums, "x", split_axis=0, concat_axis=0, tiled=True, axis_index_groups=[list(X_ORDER)]
    )
    return pl.pallas_call(
        add_kernel,
        out_shape=jax.ShapeDtypeStruct((2, FL, 2, OWN), f32),
        in_specs=[vmem],
        out_specs=vmem,
        compiler_params=params,
        name="add",
    )(sums)


def solution(mesh):
    chips = Mesh(mesh.devices.reshape(SETS, CHIPS, 2), ("wide", "x", "core"))
    columns = ("wide", "x", "core")
    return jax.shard_map(
        body,
        mesh=chips,
        in_specs=(
            P(None, None, columns),
            P(None, columns),
            P(),
            P("wide"),
            P(),
            P(columns, None),
        ),
        out_specs=P(None, None, "wide", ("x", "core")),
        check_vma=False,
    )
```
